512 devices in a mesh: ctx: 64 (over x, y, core), ch: 8 (over z).
Axes of the slice: x: 4, y: 8, z: 8, core: 2. Of those that a mesh axis runs over, the one named last changes fastest.
Arguments:
- outer_gate: bfloat16 [256, 16384], P('ch', 'ctx'), may hold values from -6 to 6
- inner_gate: bfloat16 [256, 16384], P('ch', 'ctx'), may hold values from -6 to 6
- values: bfloat16 [256, 16384], P('ch', 'ctx'), may hold values from -6 to 6
- grad_out: bfloat16 [256, 16384], P('ch', 'ctx'), may hold values from -6 to 6
- long_filter: float32 [32, 16384], P(None, 'ctx'), may hold values from -1 to 1
- mid_filter: float32 [256, 128], P('ch'), may hold values from -0.5 to 0.5
Outputs:
- grad_outer_gate: bfloat16 [256, 16384], P('ch', 'ctx')
- grad_inner_gate: bfloat16 [256, 16384], P('ch', 'ctx')
- grad_values: bfloat16 [256, 16384], P('ch', 'ctx')
- grad_long: float32 [32, 16384], P('ch', 'ctx')
- grad_mid: float32 [256, 128], P('ch')
The draws below stay inside these ranges and needn't reach their ends.
All inputs are finite; a program needn't handle non-finite values.
Results may differ from the reference program's by a relative error of at most 0.0029.
Values sent between devices are 32-bit elements; how exact they have to be, the bound alone decides.
A program may use at most 64 MiB of HBM per device.

```python
import jax
import jax.numpy as jnp

MED = 128
LENGTH = 16384
CHANNELS = 256
GROUPS = 32
N_CH = 8


def draw_long_filter(key, part):
    key = jax.random.fold_in(key, 7)
    rate_key, noise_key = jax.random.split(key)
    slowest = 2.3 / LENGTH
    fastest = 1.0 / 40.0
    spread = jax.random.uniform(rate_key, (GROUPS,), jnp.float32)
    jitter = jnp.clip(jax.random.normal(noise_key, (LENGTH, GROUPS), jnp.float32), -4.0, 4.0)
    decays = slowest * (fastest / slowest) ** spread
    positions = jnp.arange(LENGTH, dtype=jnp.float32)[:, None]
    taps = jitter * jnp.sqrt(2.0 * decays)[None, :] * jnp.exp(-decays[None, :] * positions)
    return taps.T


def level_of(stream_key, shape, shards, low, top_value):
    gain = 1.0
    for dim, parts in shards:
        draws = jax.random.uniform(jax.random.fold_in(jax.random.fold_in(stream_key, 6), dim), (parts,), jnp.float32, low / len(shards), top_value / len(shards))
        gain = gain * jnp.repeat(jnp.exp(draws), shape[dim] // parts).reshape((-1,) + (1,) * (len(shape) - 1 - dim))
    return gain


def noise(stream_key, shape, deviation, limit, pieces=(), held_as=jnp.bfloat16):
    drawn = jax.random.normal(stream_key, shape, jnp.float32) * deviation
    if len(pieces) > 0:
        drawn = level_of(stream_key, shape, pieces, -0.22, 0.18) * drawn
    return jnp.clip(drawn, min=-limit, max=limit).astype(held_as)


def setup_inputs(seed: int = 0) -> dict:
    arg_keys = jax.random.split(jax.random.key(seed), 7)
    outer_gate = noise(arg_keys[0], (CHANNELS, LENGTH), 1.0, 6.0, ((0, 8), (1, 64)))
    inner_gate = noise(arg_keys[1], (CHANNELS, LENGTH), 1.0, 6.0, ((0, 8), (1, 64)))
    values = noise(arg_keys[2], (CHANNELS, LENGTH), 1.0, 6.0, ((0, 8), (1, 64)))
    grad_out = noise(arg_keys[3], (CHANNELS, LENGTH), 1.0, 6.0, ((0, 8), (1, 64)))
    long_filter = draw_long_filter(jax.random.fold_in(arg_keys[6], 71), 0)
    mid_filter = noise(arg_keys[5], (CHANNELS, MED), MED ** -0.5, 0.5, ((0, 8),), jnp.float32)
    return dict(outer_gate=outer_gate, inner_gate=inner_gate, values=values, grad_out=grad_out, long_filter=long_filter, mid_filter=mid_filter)


def reference(outer_gate, inner_gate, values, grad_out, long_filter, mid_filter):
    outer_gate = outer_gate.T
    inner_gate = inner_gate.T
    values = values.T
    grad_out = grad_out.T
    long_filter = long_filter.T
    mid_filter = mid_filter.T
    padded_len = 2 * LENGTH
    norm_scale = LENGTH ** -0.5

    def forward(signal):
        return jnp.fft.rfft(signal, n=padded_len, axis=0)

    def inverse(spectrum_in):
        return jnp.fft.irfft(spectrum_in, n=padded_len, axis=0)[:LENGTH]

    product = inner_gate.astype(jnp.float32) * values.astype(jnp.float32)
    mid_spec = forward(mid_filter)
    prod_spec = forward(product)
    mixed = inverse(prod_spec * mid_spec)
    mix_spec = forward(mixed)
    filt_spec = forward(jnp.tile(long_filter, (1, N_CH)))
    recon_field = inverse(mix_spec * filt_spec)
    grad_full = grad_out.astype(jnp.float32)
    grad_outer = (grad_full * recon_field).astype(jnp.bfloat16)
    cot_spec = forward(grad_full * outer_gate.astype(jnp.float32))
    grad_mixed = inverse(cot_spec * jnp.conj(filt_spec))
    grad_long = inverse(cot_spec * jnp.conj(mix_spec)).reshape(LENGTH, N_CH, GROUPS).sum(1) * norm_scale
    back_spec = forward(grad_mixed)
    grad_product = inverse(back_spec * jnp.conj(mid_spec))
    grad_mid = jnp.fft.irfft(back_spec * jnp.conj(prod_spec), n=padded_len, axis=0)[:MED] * norm_scale
    grad_inner = (grad_product * values.astype(jnp.float32)).astype(jnp.bfloat16)
    grad_values = (grad_product * inner_gate.astype(jnp.float32)).astype(jnp.bfloat16)
    return grad_outer.T, grad_inner.T, grad_values.T, grad_long.astype(jnp.float32).T, grad_mid.astype(jnp.float32).T
```

```python
import functools
import math

import jax
import jax.numpy as jnp
import numpy as np
from jax import lax
from jax.experimental import pallas as pl
from jax.experimental.pallas import tpu as pltpu
from jax.sharding import PartitionSpec as P

MESH = pl.DeviceIdType.MESH
f32 = jnp.float32
bf16 = jnp.bfloat16
N = 16384
W = 128


def split_np(a):
    a = np.asarray(a, np.float32)
    hi = a.astype(jnp.bfloat16)
    lo = (a - hi.astype(np.float32)).astype(jnp.bfloat16)
    return hi, lo


def tables():
    order = np.concatenate([np.arange(0, W, 2), np.arange(1, W, 2)]).astype(np.float64)
    k = np.arange(W, dtype=np.float64)
    ang = 2.0 * math.pi * (k + 0.5)[:, None] * order[None, :] / (2 * W)
    w1 = np.concatenate([np.cos(ang), -np.sin(ang)], 0)
    w1i = w1.T / N
    tw = 2.0 * math.pi * (k + 0.5)[:, None] * k[None, :] / (2 * N)
    tc, ts = np.cos(tw), np.sin(tw)
    a2 = 2.0 * math.pi * ((k[:, None] * k[None, :]) % W) / W
    c, s = np.cos(a2), np.sin(a2)
    w2 = np.block([[c, -s], [s, c]])
    return (
        *split_np(w1),
        *split_np(w2),
        *split_np(w2.T),
        *split_np(w1i),
        tc.astype(np.float32),
        ts.astype(np.float32),
    )


def split(a):
    hi = a.astype(bf16)
    lo = (a - hi.astype(f32)).astype(bf16)
    return hi, lo


def dot(a, b, dims=(((1,), (0,)), ((), ()))):
    return lax.dot_general(a, b, dims, preferred_element_type=f32)


def dot3(a, b, dims=(((1,), (0,)), ((), ()))):
    ah, al = a
    bh, bl = b
    return dot(ah, bh, dims) + (dot(al, bh, dims) + dot(ah, bl, dims))


NT = (((1,), (1,)), ((), ()))
TN = (((0,), (0,)), ((), ()))


def kernel(
    og_h, ig_h, va_h, go_h, lf_h, mf_h, *refs
):
    tab_h = refs[:10]
    go_o, gi_o, gv_o, gl_o, gm_o = refs[10:15]
    (og, ig, va, go, lf, mf) = refs[15:21]
    tab = refs[21:31]
    (send, recv, ret, back, gls, glr) = refs[31:37]
    (in_sem, tab_sem, s1, r1, s2, r2, s3, r3, ready) = refs[37:]

    me = lax.axis_index("ctx")
    z = lax.axis_index("ch")
    l = me // 2
    core = me % 2
    zo = l // 4
    bar = pltpu.get_barrier_semaphore()

    def signal(sem, ctx, ch):
        pl.semaphore_signal(sem, inc=1, device_id=(ctx, ch), device_id_type=MESH)

    ins = [
        pltpu.make_async_copy(a, b, in_sem.at[i])
        for i, (a, b) in enumerate(
            [(ig_h, ig), (va_h, va), (go_h, go), (og_h, og), (lf_h, lf), (mf_h, mf)]
        )
    ]
    for c in ins:
        c.start()
    tabs = [pltpu.make_async_copy(a, b, tab_sem.at[i]) for i, (a, b) in enumerate(zip(tab_h, tab))]

    @pl.when(core == 1)
    def _():
        def body(i, carry):
            signal(bar, lax.rem(me + i, 64), z)
            return carry

        lax.fori_loop(1, 64, body, 0)

        @pl.when(z != zo)
        def _():
            signal(bar, me, zo)

        for c in tabs:
            c.start()

    for c in ins:
        c.wait()

    product = ig[...].astype(f32) * va[...].astype(f32)
    conv = go[...].astype(f32) * og[...].astype(f32)
    filt = lf[...]
    for r, x in enumerate((product, conv, filt, filt)):
        send[pl.ds(2 * r, 32, stride=8), :] = x[:, :W]
        send[pl.ds(2 * r + 1, 32, stride=8), :] = x[:, W:]

    @pl.when(core == 0)
    def _():
        pl.semaphore_wait(bar, 32)

    @pl.when(jnp.logical_and(core == 1, z != zo))
    def _():
        pl.semaphore_wait(bar, 31)

    @pl.when(jnp.logical_and(core == 1, z == zo))
    def _():
        pl.semaphore_wait(bar, 31 + 7)

    def tile(ref, i):
        return ref.at[pl.ds(pl.multiple_of(i * 8, 8), 8)]

    def out1(i, carry):
        chip = lax.rem(l + i, 32)
        pltpu.make_async_remote_copy(
            src_ref=tile(send, chip),
            dst_ref=tile(recv, me),
            send_sem=s1,
            recv_sem=r1,
            device_id=(2 * chip + 1, z),
            device_id_type=MESH,
        ).start()
        return carry

    lax.fori_loop(1, 32, out1, 0)

    @pl.when(core == 0)
    def _():
        out1(0, 0)

    @pl.when(core == 1)
    def _():
        pltpu.make_async_copy(tile(send, l), tile(recv, me), r1).start()
        for c in tabs:
            c.wait()
        (w1h, w1l, w2h, w2l, w3h, w3l, w4h, w4l, tcr, tsr) = tab
        w1 = (w1h[...], w1l[...])
        w2 = (w2h[...], w2l[...])
        w3 = (w3h[...], w3l[...])
        w4 = (w4h[...], w4l[...])
        tc, ts = tcr[...], tsr[...]
        row = lax.broadcasted_iota(jnp.int32, (W, W), 0)
        col = lax.broadcasted_iota(jnp.int32, (W, W), 1)
        upper = col >= row
        k = jnp.broadcast_to(mf[pl.ds(l, 1), :], (W, W))
        rolled = pltpu.roll(k, 0, 1, stride=1, stride_axis=0)
        kk = jnp.concatenate([jnp.where(upper, rolled, 0.0), jnp.where(upper, 0.0, rolled)], 1)
        kk = split(kk)

        pltpu.make_async_copy(recv, recv, r1).wait()

        @pl.when(z == zo)
        def _():
            for i in range(1, 8):
                signal(ready, me, lax.rem(z + i, 8))

        def field(r):
            return recv[pl.ds(r, 64, stride=8), :]

        half_row = lax.broadcasted_iota(jnp.int32, (64, W), 0)
        pe, po = field(0), field(1)
        po_prev = jnp.where(half_row == 0, 0.0, pltpu.roll(po, 1, 0))
        pp = jnp.concatenate(
            [jnp.concatenate([pe, po_prev], 1), jnp.concatenate([po, pe], 1)], 0
        )
        pp = split(pp)
        k0 = (kk[0][:, :W], kk[1][:, :W])
        k1 = (kk[0][:, W:], kk[1][:, W:])
        p0 = (pp[0][:, :W], pp[1][:, :W])
        p1 = (pp[0][:, W:], pp[1][:, W:])
        mixed = dot3(p0, k0) + dot3(p1, k1)
        conv_f = jnp.concatenate([field(2), field(3)], 0)
        filt_f = jnp.concatenate([field(4), field(5)], 0)
        x = jnp.concatenate([mixed, conv_f, filt_f], 1)
        s = dot3(w1, split(x))
        rows = []
        for i in range(3):
            re, im = s[:W, i * W : (i + 1) * W], s[W:, i * W : (i + 1) * W]
            rows.append(jnp.concatenate([re * tc + im * ts, im * tc - re * ts], 1))
        f = dot3(split(jnp.concatenate(rows, 0)), w2)
        mr, mi = f[:W, :W], f[:W, W:]
        cr, ci = f[W : 2 * W, :W], f[W : 2 * W, W:]
        hr, hi = f[2 * W :, :W], f[2 * W :, W:]
        y = jnp.concatenate(
            [
                jnp.concatenate([mr * hr - mi * hi, mr * hi + mi * hr], 1),
                jnp.concatenate([cr * hr + ci * hi, ci * hr - cr * hi], 1),
                jnp.concatenate([cr * mr + ci * mi, ci * mr - cr * mi], 1),
            ],
            0,
        )
        t = dot3(split(y), w3)
        cols = []
        for i in range(3):
            re, im = t[i * W : (i + 1) * W, :W], t[i * W : (i + 1) * W, W:]
            cols.append(jnp.concatenate([re * tc - im * ts, im * tc + re * ts], 0))
        out = dot3(w4, split(jnp.concatenate(cols, 1)))
        recon, gmix, glong = out[:, :W], out[:, W : 2 * W], out[:, 2 * W :] * (N**-0.5)

        gls[:, 0, :] = glong[:64]
        gls[:, 1, :] = glong[64:]

        ge, gd = gmix[:64], gmix[64:]
        ge_next = jnp.where(half_row == 63, 0.0, pltpu.roll(ge, 63, 0))
        nxt = jnp.concatenate([gd, ge_next], 0)
        gms = split(gmix)
        gprod = dot3(gms, k0, NT) + dot3(split(nxt), k1, NT)
        d0 = dot3(p0, gms, TN)
        d1 = dot3(p1, gms, TN)
        d = jnp.where(upper, d0, d1)
        for bit in range(7):
            moved = pltpu.roll(d, W - (1 << bit), 1)
            d = jnp.where((row >> bit) & 1 == 1, moved, d)
        gmid = jnp.sum(d, 0, keepdims=True) * (N**-0.5)

        ret[pl.ds(0, 64, stride=8), :] = recon[:64]
        ret[pl.ds(1, 64, stride=8), :] = recon[64:]
        ret[pl.ds(2, 64, stride=8), :] = gprod[:64]
        ret[pl.ds(3, 64, stride=8), :] = gprod[64:]
        for r in range(4, 8):
            ret[pl.ds(r, 64, stride=8), :] = jnp.broadcast_to(gmid, (64, W))

        def out2(i, carry):
            d = lax.rem(me + i, 64)
            pltpu.make_async_remote_copy(
                src_ref=tile(ret, d),
                dst_ref=tile(back, l),
                send_sem=s2,
                recv_sem=r2,
                device_id=(d, z),
                device_id_type=MESH,
            ).start()
            return carry

        lax.fori_loop(1, 64, out2, 0)
        pltpu.make_async_copy(tile(ret, me), tile(back, l), r2).start()

        @pl.when(z != zo)
        def _():
            pl.semaphore_wait(ready, 1)

        slot = z * 4 + l % 4

        def out3(i, carry):
            d = lax.rem(me + i, 64)
            pltpu.make_async_remote_copy(
                src_ref=gls.at[d],
                dst_ref=glr.at[slot],
                send_sem=s3,
                recv_sem=r3,
                device_id=(d, zo),
                device_id_type=MESH,
            ).start()
            return carry

        lax.fori_loop(1, 64, out3, 0)

        @pl.when(z != zo)
        def _():
            out3(0, 0)

        @pl.when(z == zo)
        def _():
            pltpu.make_async_copy(gls.at[me], glr.at[slot], r3).start()

    pltpu.make_async_copy(back, back, r2).wait()
    recon = jnp.concatenate([back[pl.ds(0, 32, stride=8), :], back[pl.ds(1, 32, stride=8), :]], 1)
    gprod = jnp.concatenate([back[pl.ds(2, 32, stride=8), :], back[pl.ds(3, 32, stride=8), :]], 1)
    go_o[...] = (go[...].astype(f32) * recon).astype(bf16)
    gi_o[...] = (gprod * va[...].astype(f32)).astype(bf16)
    gv_o[...] = (gprod * ig[...].astype(f32)).astype(bf16)
    gm_o[...] = back[pl.ds(4, 32, stride=8), :]
    pltpu.make_async_copy(glr, glr, r3).wait()
    total = glr[0:4]
    for i in range(1, 8):
        total = total + glr[4 * i : 4 * i + 4]
    gl_o[:, :W] = total[:, 0, :]
    gl_o[:, W:] = total[:, 1, :]

    def left(ref, count, sem):
        part = ref.at[pl.ds(0, count)]
        pltpu.make_async_copy(part, part, sem).wait()

    @pl.when(core == 0)
    def _():
        left(send, 32 * 8, s1)

    @pl.when(core == 1)
    def _():
        left(send, 31 * 8, s1)
        left(ret, 63 * 8, s2)

        @pl.when(z != zo)
        def _():
            left(gls, 64, s3)

        @pl.when(z == zo)
        def _():
            left(gls, 63, s3)


def local(outer_gate, inner_gate, values, grad_out, long_filter, mid_filter):
    tabs = tables()
    vm = pltpu.VMEM
    dma = pltpu.SemaphoreType.DMA
    any_spec = pl.BlockSpec(memory_space=pl.ANY)
    vmem_spec = pl.BlockSpec(memory_space=vm)
    ins = (outer_gate, inner_gate, values, grad_out, long_filter, mid_filter)
    return pl.pallas_call(
        kernel,
        out_shape=[
            jax.ShapeDtypeStruct((32, 256), bf16),
            jax.ShapeDtypeStruct((32, 256), bf16),
            jax.ShapeDtypeStruct((32, 256), bf16),
            jax.ShapeDtypeStruct((4, 256), f32),
            jax.ShapeDtypeStruct((32, W), f32),
        ],
        in_specs=[any_spec] * 16,
        out_specs=[vmem_spec] * 5,
        scratch_shapes=[
            *[vm((32, 256), bf16)] * 4,
            vm((32, 256), f32),
            vm((32, W), f32),
            *[vm(t.shape, t.dtype) for t in tabs],
            vm((32 * 8, W), f32),
            vm((64 * 8, W), f32),
            vm((64 * 8, W), f32),
            vm((32 * 8, W), f32),
            vm((64, 2, W), f32),
            vm((32, 2, W), f32),
            dma((6,)),
            dma((10,)),
            *[dma] * 6,
            pltpu.SemaphoreType.REGULAR,
        ],
        compiler_params=pltpu.CompilerParams(
            collective_id=0, has_side_effects=True, vmem_limit_bytes=32 * 1024 * 1024
        ),
    )(*ins, *[jnp.asarray(t) for t in tabs])


def solution(mesh):
    in_specs = (
        P("ch", "ctx"),
        P("ch", "ctx"),
        P("ch", "ctx"),
        P("ch", "ctx"),
        P(None, "ctx"),
        P("ch", None),
    )
    out_specs = (P("ch", "ctx"), P("ch", "ctx"), P("ch", "ctx"), P("ch", "ctx"), P("ch", None))
    return jax.shard_map(local, mesh=mesh, in_specs=in_specs, out_specs=out_specs, check_vma=False)
```

```python
import functools
import math

import jax
import jax.numpy as jnp
import numpy as np
from jax import lax
from jax.experimental import pallas as pl
from jax.experimental.pallas import tpu as pltpu
from jax.sharding import PartitionSpec as P

MESH = pl.DeviceIdType.MESH
f32 = jnp.float32
bf16 = jnp.bfloat16
N = 16384
W = 128


def split_np(a):
    a = np.asarray(a, np.float32)
    hi = a.astype(jnp.bfloat16)
    lo = (a - hi.astype(np.float32)).astype(jnp.bfloat16)
    return hi, lo


def tables():
    order = np.concatenate([np.arange(0, W, 2), np.arange(1, W, 2)]).astype(np.float64)
    k = np.arange(W, dtype=np.float64)
    ang = 2.0 * math.pi * (k + 0.5)[:, None] * order[None, :] / (2 * W)
    w1 = np.concatenate([np.cos(ang), -np.sin(ang)], 0)
    w1i = w1.T / N
    tw = 2.0 * math.pi * (k + 0.5)[:, None] * k[None, :] / (2 * N)
    tc, ts = np.cos(tw), np.sin(tw)
    a2 = 2.0 * math.pi * ((k[:, None] * k[None, :]) % W) / W
    c, s = np.cos(a2), np.sin(a2)
    w2 = np.block([[c, -s], [s, c]])
    return (
        *split_np(w1),
        *split_np(w2),
        *split_np(w2.T),
        *split_np(w1i),
        tc.astype(np.float32),
        ts.astype(np.float32),
    )


def split(a):
    hi = a.astype(bf16)
    lo = (a - hi.astype(f32)).astype(bf16)
    return hi, lo


def dot(a, b, dims=(((1,), (0,)), ((), ()))):
    return lax.dot_general(a, b, dims, preferred_element_type=f32)


def dot3(a, b, dims=(((1,), (0,)), ((), ()))):
    ah, al = a
    bh, bl = b
    return dot(ah, bh, dims) + (dot(al, bh, dims) + dot(ah, bl, dims))


NT = (((1,), (1,)), ((), ()))
TN = (((0,), (0,)), ((), ()))


def ring(d, n):
    return min(d, n - d)


OFFSETS = sorted(
    [(dx, dy) for dx in range(4) for dy in range(8)], key=lambda o: -(ring(o[0], 4) + ring(o[1], 8))
)


def kernel(og_h, ig_h, va_h, go_h, lf_h, mf_h, *refs):
    tab_h = refs[:10]
    outs_h = refs[10:14]
    glr = refs[14]
    (og, ig, va, go, lf, mf) = refs[15:21]
    tab = refs[21:31]
    outs = refs[31:35]
    go_o, gi_o, gv_o, gm_o = outs
    (send, recv, ret, back, gls) = refs[35:40]
    (in_sem, tab_sem, out_sem, s1, r1, s2, r2, s3, r3, ready) = refs[40:]

    me = lax.axis_index("ctx")
    z = lax.axis_index("ch")
    l = me // 2
    px, py = l // 8, l % 8
    works = me % 2 == 1
    zo = l // 4
    hub = z == zo
    bar = pltpu.get_barrier_semaphore()

    def signal(sem, ctx, ch):
        pl.semaphore_signal(sem, inc=1, device_id=(ctx, ch), device_id_type=MESH)

    def chip_at(dx, dy):
        return lax.rem(px + dx, 4) * 8 + lax.rem(py + dy, 8)

    ins = [
        pltpu.make_async_copy(a, b, in_sem.at[i])
        for i, (a, b) in enumerate(
            [(ig_h, ig), (va_h, va), (go_h, go), (og_h, og), (lf_h, lf), (mf_h, mf)]
        )
    ]
    for c in ins:
        c.start()
    tabs = [pltpu.make_async_copy(a, b, tab_sem.at[i]) for i, (a, b) in enumerate(zip(tab_h, tab))]

    @pl.when(works)
    def _():
        for dx, dy in OFFSETS:
            chip = chip_at(dx, dy)
            signal(bar, 2 * chip, z)
            if (dx, dy) != (0, 0):
                signal(bar, 2 * chip + 1, z)

        @pl.when(jnp.logical_not(hub))
        def _():
            signal(bar, me, zo)

        for c in tabs:
            c.start()

    for c in ins:
        c.wait()

    product = ig[...].astype(f32) * va[...].astype(f32)
    conv = go[...].astype(f32) * og[...].astype(f32)
    filt = lf[...]
    for r, x in enumerate((product, conv, filt, filt)):
        send[pl.ds(2 * r, 32, stride=8), :] = x[:, :W]
        send[pl.ds(2 * r + 1, 32, stride=8), :] = x[:, W:]

    @pl.when(jnp.logical_not(works))
    def _():
        pl.semaphore_wait(bar, 32)

    @pl.when(jnp.logical_and(works, jnp.logical_not(hub)))
    def _():
        pl.semaphore_wait(bar, 31)

    @pl.when(jnp.logical_and(works, hub))
    def _():
        pl.semaphore_wait(bar, 38)

    def tile(ref, i):
        return ref.at[pl.ds(pl.multiple_of(i * 8, 8), 8)]

    def out1(chip):
        pltpu.make_async_remote_copy(
            src_ref=tile(send, chip),
            dst_ref=tile(recv, me),
            send_sem=s1,
            recv_sem=r1,
            device_id=(2 * chip + 1, z),
            device_id_type=MESH,
        ).start()

    for dx, dy in OFFSETS[:-1]:
        out1(chip_at(dx, dy))

    @pl.when(jnp.logical_not(works))
    def _():
        out1(l)

    @pl.when(works)
    def _():
        pltpu.make_async_copy(tile(send, l), tile(recv, me), r1).start()
        for c in tabs:
            c.wait()
        (w1h, w1l, w2h, w2l, w3h, w3l, w4h, w4l, tcr, tsr) = tab
        w1 = (w1h[...], w1l[...])
        w2 = (w2h[...], w2l[...])
        w3 = (w3h[...], w3l[...])
        w4 = (w4h[...], w4l[...])
        tc, ts = tcr[...], tsr[...]
        row = lax.broadcasted_iota(jnp.int32, (W, W), 0)
        col = lax.broadcasted_iota(jnp.int32, (W, W), 1)
        upper = col >= row
        half_row = lax.broadcasted_iota(jnp.int32, (64, W), 0)
        k = jnp.broadcast_to(mf[pl.ds(l, 1), :], (W, W))
        rolled = pltpu.roll(k, 0, 1, stride=1, stride_axis=0)
        k0 = split(jnp.where(upper, rolled, 0.0))
        k1 = split(jnp.where(upper, 0.0, rolled))

        pltpu.make_async_copy(recv, recv, r1).wait()

        @pl.when(hub)
        def _():
            for i in (4, 3, 5, 2, 6, 1, 7):
                signal(ready, me, lax.rem(z + i, 8))

        def field(r):
            return recv[pl.ds(r, 64, stride=8), :]

        def both(r):
            return jnp.concatenate([field(r), field(r + 1)], 0)

        def forward(x):
            s = dot3(w1, split(x))
            parts = []
            for i in range(x.shape[1] // W):
                re, im = s[:W, i * W : (i + 1) * W], s[W:, i * W : (i + 1) * W]
                parts.append(jnp.concatenate([re * tc + im * ts, im * tc - re * ts], 1))
            return dot3(split(jnp.concatenate(parts, 0)), w2)

        def inverse(y):
            t = dot3(split(y), w3)
            parts = []
            for i in range(y.shape[0] // W):
                re, im = t[i * W : (i + 1) * W, :W], t[i * W : (i + 1) * W, W:]
                parts.append(jnp.concatenate([re * tc - im * ts, im * tc + re * ts], 0))
            return dot3(w4, split(jnp.concatenate(parts, 1)))

        pe, po = field(0), field(1)
        po_prev = jnp.where(half_row == 0, 0.0, pltpu.roll(po, 1, 0))
        p0 = split(jnp.concatenate([pe, po], 0))
        p1 = split(jnp.concatenate([po_prev, pe], 0))
        mixed = dot3(p0, k0) + dot3(p1, k1)
        f = forward(jnp.concatenate([mixed, both(2)], 1))
        mr, mi = f[:W, :W], f[:W, W:]
        cr, ci = f[W:, :W], f[W:, W:]
        glong = inverse(jnp.concatenate([cr * mr + ci * mi, ci * mr - cr * mi], 1)) * (N**-0.5)
        gls[:, 0, :] = glong[:64]
        gls[:, 1, :] = glong[64:]

        @pl.when(jnp.logical_not(hub))
        def _():
            pl.semaphore_wait(ready, 1)

        slot = z * 4 + l % 4

        def out3(d):
            pltpu.make_async_remote_copy(
                src_ref=gls.at[d],
                dst_ref=glr.at[slot],
                send_sem=s3,
                recv_sem=r3,
                device_id=(d, zo),
                device_id_type=MESH,
            ).start()

        for dx, dy in OFFSETS:
            chip = chip_at(dx, dy)
            out3(2 * chip)
            if (dx, dy) != (0, 0):
                out3(2 * chip + 1)

        @pl.when(jnp.logical_not(hub))
        def _():
            out3(me)

        @pl.when(hub)
        def _():
            pltpu.make_async_copy(gls.at[me], glr.at[slot], r3).start()

        h = forward(both(4))
        hr, hi = h[:, :W], h[:, W:]
        out = inverse(
            jnp.concatenate(
                [
                    jnp.concatenate([mr * hr - mi * hi, mr * hi + mi * hr], 1),
                    jnp.concatenate([cr * hr + ci * hi, ci * hr - cr * hi], 1),
                ],
                0,
            )
        )
        recon, gmix = out[:, :W], out[:, W:]
        ge, gd = gmix[:64], gmix[64:]
        ge_next = jnp.where(half_row == 63, 0.0, pltpu.roll(ge, 63, 0))
        gms = split(gmix)
        gprod = dot3(gms, k0, NT) + dot3(split(jnp.concatenate([gd, ge_next], 0)), k1, NT)
        d = jnp.where(upper, dot3(p0, gms, TN), dot3(p1, gms, TN))
        for bit in range(7):
            moved = pltpu.roll(d, W - (1 << bit), 1)
            d = jnp.where((row >> bit) & 1 == 1, moved, d)
        gmid = jnp.sum(d, 0, keepdims=True) * (N**-0.5)

        ret[pl.ds(0, 64, stride=8), :] = recon[:64]
        ret[pl.ds(1, 64, stride=8), :] = recon[64:]
        ret[pl.ds(2, 64, stride=8), :] = gprod[:64]
        ret[pl.ds(3, 64, stride=8), :] = gprod[64:]
        for r in range(4, 8):
            ret[pl.ds(r, 64, stride=8), :] = jnp.broadcast_to(gmid, (64, W))

        def out2(d):
            pltpu.make_async_remote_copy(
                src_ref=tile(ret, d),
                dst_ref=tile(back, l),
                send_sem=s2,
                recv_sem=r2,
                device_id=(d, z),
                device_id_type=MESH,
            ).start()

        for dx, dy in OFFSETS:
            chip = chip_at(dx, dy)
            out2(2 * chip)
            if (dx, dy) != (0, 0):
                out2(2 * chip + 1)
        pltpu.make_async_copy(tile(ret, me), tile(back, l), r2).start()

    def left(ref, count, sem):
        part = ref.at[pl.ds(0, count)]
        pltpu.make_async_copy(part, part, sem).wait()

    left(send, 31 * 8, s1)

    @pl.when(jnp.logical_not(works))
    def _():
        left(send, 8, s1)

    @pl.when(works)
    def _():
        left(gls, 63, s3)
        left(ret, 63 * 8, s2)

        @pl.when(jnp.logical_not(hub))
        def _():
            left(gls, 1, s3)

    pltpu.make_async_copy(back, back, r2).wait()

    def rows(r):
        return back[pl.ds(r, 32, stride=8), :]

    recon = jnp.concatenate([rows(0), rows(1)], 1)
    gprod = jnp.concatenate([rows(2), rows(3)], 1)
    go_o[...] = (go[...].astype(f32) * recon).astype(bf16)
    gi_o[...] = (gprod * va[...].astype(f32)).astype(bf16)
    gv_o[...] = (gprod * ig[...].astype(f32)).astype(bf16)
    gm_o[...] = rows(4)
    leave = [pltpu.make_async_copy(a, b, out_sem.at[i]) for i, (a, b) in enumerate(zip(outs, outs_h))]
    for c in leave:
        c.start()
    for c in leave:
        c.wait()
    pltpu.make_async_copy(glr, glr, r3).wait()


def deliver(a, b, c, m, parts, a_o, b_o, c_o, gl_o, m_o):
    a_o[...] = a[...]
    b_o[...] = b[...]
    c_o[...] = c[...]
    m_o[...] = m[...]
    total = parts[0:4]
    for i in range(1, 8):
        total = total + parts[4 * i : 4 * i + 4]
    gl_o[:, :W] = total[:, 0, :]
    gl_o[:, W:] = total[:, 1, :]


def local(outer_gate, inner_gate, values, grad_out, long_filter, mid_filter):
    tabs = tables()
    vm = pltpu.VMEM
    dma = pltpu.SemaphoreType.DMA
    hbm = pl.BlockSpec(memory_space=pl.ANY)
    vmem = pl.BlockSpec(memory_space=vm)
    ins = (outer_gate, inner_gate, values, grad_out, long_filter, mid_filter)
    outs = [((32, 256), bf16)] * 3 + [((32, W), f32)]
    shapes = [jax.ShapeDtypeStruct(*o) for o in outs]
    results = pl.pallas_call(
        kernel,
        out_shape=[*shapes, jax.ShapeDtypeStruct((32, 2, W), f32)],
        in_specs=[hbm] * 16,
        out_specs=[hbm] * 5,
        scratch_shapes=[
            *[vm((32, 256), bf16)] * 4,
            vm((32, 256), f32),
            vm((32, W), f32),
            *[vm(t.shape, t.dtype) for t in tabs],
            *[vm(*o) for o in outs],
            vm((32 * 8, W), f32),
            vm((64 * 8, W), f32),
            vm((64 * 8, W), f32),
            vm((32 * 8, W), f32),
            vm((64, 2, W), f32),
            dma((6,)),
            dma((10,)),
            dma((4,)),
            *[dma] * 6,
            pltpu.SemaphoreType.REGULAR,
        ],
        compiler_params=pltpu.CompilerParams(collective_id=0, has_side_effects=True),
    )(*ins, *[jnp.asarray(t) for t in tabs])
    return pl.pallas_call(
        deliver,
        out_shape=[*shapes[:3], jax.ShapeDtypeStruct((4, 256), f32), shapes[3]],
        in_specs=[vmem] * 5,
        out_specs=[vmem] * 5,
    )(*results)


def solution(mesh):
    in_specs = (
        P("ch", "ctx"),
        P("ch", "ctx"),
        P("ch", "ctx"),
        P("ch", "ctx"),
        P(None, "ctx"),
        P("ch", None),
    )
    out_specs = (P("ch", "ctx"), P("ch", "ctx"), P("ch", "ctx"), P("ch", "ctx"), P("ch", None))
    return jax.shard_map(local, mesh=mesh, in_specs=in_specs, out_specs=out_specs, check_vma=False)
```

```python
import functools
import math

import jax
import jax.numpy as jnp
import numpy as np
from jax import lax
from jax.experimental import pallas as pl
from jax.experimental.pallas import tpu as pltpu
from jax.sharding import PartitionSpec as P

MESH = pl.DeviceIdType.MESH
f32 = jnp.float32
bf16 = jnp.bfloat16
N = 16384
W = 128


def split_np(a):
    a = np.asarray(a, np.float32)
    hi = a.astype(jnp.bfloat16)
    lo = (a - hi.astype(np.float32)).astype(jnp.bfloat16)
    return hi, lo


def tables():
    order = np.concatenate([np.arange(0, W, 2), np.arange(1, W, 2)]).astype(np.float64)
    k = np.arange(W, dtype=np.float64)
    ang = 2.0 * math.pi * (k + 0.5)[:, None] * order[None, :] / (2 * W)
    w1 = np.concatenate([np.cos(ang), -np.sin(ang)], 0)
    w1i = w1.T / N
    tw = 2.0 * math.pi * (k + 0.5)[:, None] * k[None, :] / (2 * N)
    tc, ts = np.cos(tw), np.sin(tw)
    a2 = 2.0 * math.pi * ((k[:, None] * k[None, :]) % W) / W
    c, s = np.cos(a2), np.sin(a2)
    w2 = np.block([[c, -s], [s, c]])
    return (
        *split_np(w1),
        *split_np(w2),
        *split_np(w2.T),
        *split_np(w1i),
        tc.astype(np.float32),
        ts.astype(np.float32),
    )


def split(a):
    hi = a.astype(bf16)
    lo = (a - hi.astype(f32)).astype(bf16)
    return hi, lo


def dot(a, b, dims=(((1,), (0,)), ((), ()))):
    return lax.dot_general(a, b, dims, preferred_element_type=f32)


def dot3(a, b, dims=(((1,), (0,)), ((), ()))):
    ah, al = a
    bh, bl = b
    return dot(ah, bh, dims) + (dot(al, bh, dims) + dot(ah, bl, dims))


NT = (((1,), (1,)), ((), ()))
TN = (((0,), (0,)), ((), ()))


def ring(d, n):
    return min(d, n - d)


OFFSETS = sorted(
    [(dx, dy) for dx in range(4) for dy in range(8)], key=lambda o: -(ring(o[0], 4) + ring(o[1], 8))
)


def kernel(og_h, ig_h, va_h, go_h, lf_h, mf_h, *refs):
    tab_h = refs[:10]
    outs_h = refs[10:14]
    glr = refs[14]
    (og, ig, va, go, lf, mf) = refs[15:21]
    tab = refs[21:31]
    outs = refs[31:35]
    go_o, gi_o, gv_o, gm_o = outs
    (send, recv, send_f, recv_f, ret, back, gls) = refs[35:42]
    (in_sem, tab_sem, out_sem, s1, r1, s2, r2, s3, r3, s4, r4, ready) = refs[42:]

    me = lax.axis_index("ctx")
    z = lax.axis_index("ch")
    l = me // 2
    px, py = l // 8, l % 8
    works = me % 2 == 1
    zo = l // 4
    hub = z == zo
    bar = pltpu.get_barrier_semaphore()

    def signal(sem, ctx, ch):
        pl.semaphore_signal(sem, inc=1, device_id=(ctx, ch), device_id_type=MESH)

    def chip_at(dx, dy):
        return lax.rem(px + dx, 4) * 8 + lax.rem(py + dy, 8)

    ins = [
        pltpu.make_async_copy(a, b, in_sem.at[i])
        for i, (a, b) in enumerate(
            [(ig_h, ig), (va_h, va), (go_h, go), (og_h, og), (lf_h, lf), (mf_h, mf)]
        )
    ]
    for c in ins:
        c.start()
    tabs = [pltpu.make_async_copy(a, b, tab_sem.at[i]) for i, (a, b) in enumerate(zip(tab_h, tab))]

    @pl.when(works)
    def _():
        for dx, dy in OFFSETS:
            chip = chip_at(dx, dy)
            signal(bar, 2 * chip, z)
            if (dx, dy) != (0, 0):
                signal(bar, 2 * chip + 1, z)

        @pl.when(jnp.logical_not(hub))
        def _():
            signal(bar, me, zo)

        for c in tabs:
            c.start()

    for c in ins:
        c.wait()

    product = ig[...].astype(f32) * va[...].astype(f32)
    conv = go[...].astype(f32) * og[...].astype(f32)
    filt = lf[...]
    send[:, 0, :] = product[:, :W]
    send[:, 1, :] = product[:, W:]
    send[:, 2, :] = conv[:, :W]
    send[:, 3, :] = conv[:, W:]
    send_f[:, 0, :] = filt[:, :W]
    send_f[:, 1, :] = filt[:, W:]

    @pl.when(jnp.logical_not(works))
    def _():
        pl.semaphore_wait(bar, 32)

    @pl.when(jnp.logical_and(works, jnp.logical_not(hub)))
    def _():
        pl.semaphore_wait(bar, 31)

    @pl.when(jnp.logical_and(works, hub))
    def _():
        pl.semaphore_wait(bar, 38)

    def tile(ref, i):
        return ref.at[pl.ds(pl.multiple_of(i * 8, 8), 8)]

    def out(src, dst, ssem, rsem, d, p):
        pltpu.make_async_remote_copy(
            src_ref=src,
            dst_ref=dst,
            send_sem=ssem,
            recv_sem=rsem,
            device_id=(d, p),
            device_id_type=MESH,
        ).start()

    def out_tokens(chip):
        out(send.at[chip], recv.at[me], s1, r1, 2 * chip + 1, z)

    def out_filter(chip):
        out(send_f.at[chip], recv_f.at[me], s4, r4, 2 * chip + 1, z)

    for put in (out_tokens, out_filter):
        for dx, dy in OFFSETS[:-1]:
            put(chip_at(dx, dy))

    @pl.when(jnp.logical_not(works))
    def _():
        out_tokens(l)
        out_filter(l)

    @pl.when(works)
    def _():
        pltpu.make_async_copy(send.at[l], recv.at[me], r1).start()
        pltpu.make_async_copy(send_f.at[l], recv_f.at[me], r4).start()
        for c in tabs:
            c.wait()
        (w1h, w1l, w2h, w2l, w3h, w3l, w4h, w4l, tcr, tsr) = tab
        w1 = (w1h[...], w1l[...])
        w2 = (w2h[...], w2l[...])
        w3 = (w3h[...], w3l[...])
        w4 = (w4h[...], w4l[...])
        tc, ts = tcr[...], tsr[...]
        row = lax.broadcasted_iota(jnp.int32, (W, W), 0)
        col = lax.broadcasted_iota(jnp.int32, (W, W), 1)
        upper = col >= row
        half_row = lax.broadcasted_iota(jnp.int32, (64, W), 0)
        k = jnp.broadcast_to(mf[pl.ds(l, 1), :], (W, W))
        rolled = pltpu.roll(k, 0, 1, stride=1, stride_axis=0)
        k0 = split(jnp.where(upper, rolled, 0.0))
        k1 = split(jnp.where(upper, 0.0, rolled))

        pltpu.make_async_copy(recv, recv, r1).wait()

        @pl.when(hub)
        def _():
            for i in (4, 3, 5, 2, 6, 1, 7):
                signal(ready, me, lax.rem(z + i, 8))

        def forward(x):
            s = dot3(w1, split(x))
            parts = []
            for i in range(x.shape[1] // W):
                re, im = s[:W, i * W : (i + 1) * W], s[W:, i * W : (i + 1) * W]
                parts.append(jnp.concatenate([re * tc + im * ts, im * tc - re * ts], 1))
            return dot3(split(jnp.concatenate(parts, 0)), w2)

        def inverse(y):
            t = dot3(split(y), w3)
            parts = []
            for i in range(y.shape[0] // W):
                re, im = t[i * W : (i + 1) * W, :W], t[i * W : (i + 1) * W, W:]
                parts.append(jnp.concatenate([re * tc - im * ts, im * tc + re * ts], 0))
            return dot3(w4, split(jnp.concatenate(parts, 1)))

        pe, po = recv[:, 0, :], recv[:, 1, :]
        po_prev = jnp.where(half_row == 0, 0.0, pltpu.roll(po, 1, 0))
        p0 = split(jnp.concatenate([pe, po], 0))
        p1 = split(jnp.concatenate([po_prev, pe], 0))
        mixed = dot3(p0, k0) + dot3(p1, k1)
        conv_f = jnp.concatenate([recv[:, 2, :], recv[:, 3, :]], 0)
        f = forward(jnp.concatenate([mixed, conv_f], 1))
        mr, mi = f[:W, :W], f[:W, W:]
        cr, ci = f[W:, :W], f[W:, W:]
        glong = inverse(jnp.concatenate([cr * mr + ci * mi, ci * mr - cr * mi], 1)) * (N**-0.5)
        gls[:, 0, :] = glong[:64]
        gls[:, 1, :] = glong[64:]

        slot = z * 4 + l % 4

        def out_long():
            @pl.when(jnp.logical_not(hub))
            def _():
                pl.semaphore_wait(ready, 1)

            for dx, dy in OFFSETS:
                d = 2 * chip_at(dx, dy)
                out(gls.at[d], glr.at[slot], s3, r3, d, zo)
                if (dx, dy) != (0, 0):
                    out(gls.at[d + 1], glr.at[slot], s3, r3, d + 1, zo)

            @pl.when(jnp.logical_not(hub))
            def _():
                out(gls.at[me], glr.at[slot], s3, r3, me, zo)

            @pl.when(hub)
            def _():
                pltpu.make_async_copy(gls.at[me], glr.at[slot], r3).start()

        @pl.when(z >= zo)
        def _():
            out_long()

        pltpu.make_async_copy(recv_f, recv_f, r4).wait()
        h = forward(jnp.concatenate([recv_f[:, 0, :], recv_f[:, 1, :]], 0))
        hr, hi = h[:, :W], h[:, W:]
        both = inverse(
            jnp.concatenate(
                [
                    jnp.concatenate([mr * hr - mi * hi, mr * hi + mi * hr], 1),
                    jnp.concatenate([cr * hr + ci * hi, ci * hr - cr * hi], 1),
                ],
                0,
            )
        )
        recon, gmix = both[:, :W], both[:, W:]
        ge, gd = gmix[:64], gmix[64:]
        ge_next = jnp.where(half_row == 63, 0.0, pltpu.roll(ge, 63, 0))
        gms = split(gmix)
        gprod = dot3(gms, k0, NT) + dot3(split(jnp.concatenate([gd, ge_next], 0)), k1, NT)
        d = jnp.where(upper, dot3(p0, gms, TN), dot3(p1, gms, TN))
        for bit in range(7):
            moved = pltpu.roll(d, W - (1 << bit), 1)
            d = jnp.where((row >> bit) & 1 == 1, moved, d)
        gmid = jnp.sum(d, 0, keepdims=True) * (N**-0.5)

        ret[pl.ds(0, 64, stride=8), :] = recon[:64]
        ret[pl.ds(1, 64, stride=8), :] = recon[64:]
        ret[pl.ds(2, 64, stride=8), :] = gprod[:64]
        ret[pl.ds(3, 64, stride=8), :] = gprod[64:]
        for r in range(4, 8):
            ret[pl.ds(r, 64, stride=8), :] = jnp.broadcast_to(gmid, (64, W))

        for dx, dy in OFFSETS:
            d = 2 * chip_at(dx, dy)
            out(tile(ret, d), tile(back, l), s2, r2, d, z)
            if (dx, dy) != (0, 0):
                out(tile(ret, d + 1), tile(back, l), s2, r2, d + 1, z)
        pltpu.make_async_copy(tile(ret, me), tile(back, l), r2).start()

        @pl.when(z < zo)
        def _():
            out_long()

    def left(ref, count, sem):
        part = ref.at[pl.ds(0, count)]
        pltpu.make_async_copy(part, part, sem).wait()

    left(send, 31, s1)
    left(send_f, 31, s4)

    @pl.when(jnp.logical_not(works))
    def _():
        left(send, 1, s1)
        left(send_f, 1, s4)

    @pl.when(works)
    def _():
        left(gls, 63, s3)
        left(ret, 63 * 8, s2)

        @pl.when(jnp.logical_not(hub))
        def _():
            left(gls, 1, s3)

    pltpu.make_async_copy(back, back, r2).wait()

    def rows(r):
        return back[pl.ds(r, 32, stride=8), :]

    recon = jnp.concatenate([rows(0), rows(1)], 1)
    gprod = jnp.concatenate([rows(2), rows(3)], 1)
    go_o[...] = (go[...].astype(f32) * recon).astype(bf16)
    gi_o[...] = (gprod * va[...].astype(f32)).astype(bf16)
    gv_o[...] = (gprod * ig[...].astype(f32)).astype(bf16)
    gm_o[...] = rows(4)
    leave = [pltpu.make_async_copy(a, b, out_sem.at[i]) for i, (a, b) in enumerate(zip(outs, outs_h))]
    for c in leave:
        c.start()
    for c in leave:
        c.wait()
    pltpu.make_async_copy(glr, glr, r3).wait()


def deliver(a, b, c, m, parts, a_o, b_o, c_o, gl_o, m_o):
    a_o[...] = a[...]
    b_o[...] = b[...]
    c_o[...] = c[...]
    m_o[...] = m[...]
    total = parts[0:4]
    for i in range(1, 8):
        total = total + parts[4 * i : 4 * i + 4]
    gl_o[:, :W] = total[:, 0, :]
    gl_o[:, W:] = total[:, 1, :]


def local(outer_gate, inner_gate, values, grad_out, long_filter, mid_filter):
    tabs = tables()
    vm = pltpu.VMEM
    dma = pltpu.SemaphoreType.DMA
    hbm = pl.BlockSpec(memory_space=pl.ANY)
    vmem = pl.BlockSpec(memory_space=vm)
    ins = (outer_gate, inner_gate, values, grad_out, long_filter, mid_filter)
    outs = [((32, 256), bf16)] * 3 + [((32, W), f32)]
    shapes = [jax.ShapeDtypeStruct(*o) for o in outs]
    results = pl.pallas_call(
        kernel,
        out_shape=[*shapes, jax.ShapeDtypeStruct((32, 2, W), f32)],
        in_specs=[hbm] * 16,
        out_specs=[hbm] * 5,
        scratch_shapes=[
            *[vm((32, 256), bf16)] * 4,
            vm((32, 256), f32),
            vm((32, W), f32),
            *[vm(t.shape, t.dtype) for t in tabs],
            *[vm(*o) for o in outs],
            vm((32, 4, W), f32),
            vm((64, 4, W), f32),
            vm((32, 2, W), f32),
            vm((64, 2, W), f32),
            vm((64 * 8, W), f32),
            vm((32 * 8, W), f32),
            vm((64, 2, W), f32),
            dma((6,)),
            dma((10,)),
            dma((4,)),
            *[dma] * 8,
            pltpu.SemaphoreType.REGULAR,
        ],
        compiler_params=pltpu.CompilerParams(collective_id=0, has_side_effects=True),
    )(*ins, *[jnp.asarray(t) for t in tabs])
    return pl.pallas_call(
        deliver,
        out_shape=[*shapes[:3], jax.ShapeDtypeStruct((4, 256), f32), shapes[3]],
        in_specs=[vmem] * 5,
        out_specs=[vmem] * 5,
    )(*results)


def solution(mesh):
    in_specs = (
        P("ch", "ctx"),
        P("ch", "ctx"),
        P("ch", "ctx"),
        P("ch", "ctx"),
        P(None, "ctx"),
        P("ch", None),
    )
    out_specs = (P("ch", "ctx"), P("ch", "ctx"), P("ch", "ctx"), P("ch", "ctx"), P("ch", None))
    return jax.shard_map(local, mesh=mesh, in_specs=in_specs, out_specs=out_specs, check_vma=False)
```

```python
import functools
import math

import jax
import jax.numpy as jnp
import numpy as np
from jax import lax
from jax.experimental import pallas as pl
from jax.experimental.pallas import tpu as pltpu
from jax.sharding import PartitionSpec as P

MESH = pl.DeviceIdType.MESH
f32 = jnp.float32
bf16 = jnp.bfloat16
N = 16384
VMEM_BYTES = 16 * 1024 * 1024
W = 128


def split_np(a):
    a = np.asarray(a, np.float32)
    hi = a.astype(jnp.bfloat16)
    lo = (a - hi.astype(np.float32)).astype(jnp.bfloat16)
    return hi, lo


def tables():
    order = np.concatenate([np.arange(0, W, 2), np.arange(1, W, 2)]).astype(np.float64)
    k = np.arange(W, dtype=np.float64)
    ang = 2.0 * math.pi * (k + 0.5)[:, None] * order[None, :] / (2 * W)
    w1 = np.concatenate([np.cos(ang), -np.sin(ang)], 0)
    w1i = w1.T / N
    tw = 2.0 * math.pi * (k + 0.5)[:, None] * k[None, :] / (2 * N)
    tc, ts = np.cos(tw), np.sin(tw)
    a2 = 2.0 * math.pi * ((k[:, None] * k[None, :]) % W) / W
    c, s = np.cos(a2), np.sin(a2)
    w2 = np.block([[c, -s], [s, c]])
    return (
        *split_np(w1),
        *split_np(w2),
        *split_np(w2.T),
        *split_np(w1i),
        tc.astype(np.float32),
        ts.astype(np.float32),
    )


def split(a):
    hi = a.astype(bf16)
    lo = (a - hi.astype(f32)).astype(bf16)
    return hi, lo


def dot(a, b, dims=(((1,), (0,)), ((), ()))):
    return lax.dot_general(a, b, dims, preferred_element_type=f32)


def dot3(a, b, dims=(((1,), (0,)), ((), ()))):
    ah, al = a
    bh, bl = b
    return dot(ah, bh, dims) + (dot(al, bh, dims) + dot(ah, bl, dims))


NT = (((1,), (1,)), ((), ()))
TN = (((0,), (0,)), ((), ()))


def ring(d, n):
    return min(d, n - d)


OFFSETS = sorted(
    [(dx, dy) for dx in range(4) for dy in range(8)], key=lambda o: -(ring(o[0], 4) + ring(o[1], 8))
)


def kernel(og_h, ig_h, va_h, go_h, lf_h, mf_h, *refs):
    tab_h = refs[:10]
    (go_o, gi_o, gv_o, gm_o, glr) = refs[10:15]
    (og, ig, va, go, lf, mf) = refs[15:21]
    tab = refs[21:31]
    (send, recv, send_f, recv_f, ret, back, gls) = refs[31:38]
    (in_sem, tab_sem, s1, r1, s2, r2, s3, r3, s4, r4, ready) = refs[38:]

    me = lax.axis_index("ctx")
    z = lax.axis_index("ch")
    l = me // 2
    px, py = l // 8, l % 8
    works = me % 2 == 1
    zo = l // 4
    hub = z == zo
    bar = pltpu.get_barrier_semaphore()

    def signal(sem, ctx, ch):
        pl.semaphore_signal(sem, inc=1, device_id=(ctx, ch), device_id_type=MESH)

    def chip_at(dx, dy):
        return lax.rem(px + dx, 4) * 8 + lax.rem(py + dy, 8)

    ins = [
        pltpu.make_async_copy(a, b, in_sem.at[i])
        for i, (a, b) in enumerate(
            [(ig_h, ig), (va_h, va), (go_h, go), (og_h, og), (lf_h, lf), (mf_h, mf)]
        )
    ]
    for c in ins:
        c.start()
    tabs = [pltpu.make_async_copy(a, b, tab_sem.at[i]) for i, (a, b) in enumerate(zip(tab_h, tab))]

    @pl.when(works)
    def _():
        for dx, dy in OFFSETS:
            chip = chip_at(dx, dy)
            signal(bar, 2 * chip, z)
            if (dx, dy) != (0, 0):
                signal(bar, 2 * chip + 1, z)

        @pl.when(jnp.logical_not(hub))
        def _():
            signal(bar, me, zo)

        for c in tabs:
            c.start()

    for c in ins:
        c.wait()

    product = ig[...].astype(f32) * va[...].astype(f32)
    conv = go[...].astype(f32) * og[...].astype(f32)
    filt = lf[...]
    send[:, 0, :] = product[:, :W]
    send[:, 1, :] = product[:, W:]
    send[:, 2, :] = conv[:, :W]
    send[:, 3, :] = conv[:, W:]
    send_f[:, 0, :] = filt[:, :W]
    send_f[:, 1, :] = filt[:, W:]

    @pl.when(jnp.logical_not(works))
    def _():
        pl.semaphore_wait(bar, 32)

    @pl.when(jnp.logical_and(works, jnp.logical_not(hub)))
    def _():
        pl.semaphore_wait(bar, 31)

    @pl.when(jnp.logical_and(works, hub))
    def _():
        pl.semaphore_wait(bar, 38)

    def tile(ref, i):
        return ref.at[pl.ds(pl.multiple_of(i * 8, 8), 8)]

    def out(src, dst, ssem, rsem, d, p):
        pltpu.make_async_remote_copy(
            src_ref=src,
            dst_ref=dst,
            send_sem=ssem,
            recv_sem=rsem,
            device_id=(d, p),
            device_id_type=MESH,
        ).start()

    def out_tokens(chip):
        out(send.at[chip], recv.at[me], s1, r1, 2 * chip + 1, z)

    def out_filter(chip):
        out(send_f.at[chip], recv_f.at[me], s4, r4, 2 * chip + 1, z)

    for put in (out_tokens, out_filter):
        for dx, dy in OFFSETS[:-1]:
            put(chip_at(dx, dy))

    @pl.when(jnp.logical_not(works))
    def _():
        out_tokens(l)
        out_filter(l)

    @pl.when(works)
    def _():
        pltpu.make_async_copy(send.at[l], recv.at[me], r1).start()
        pltpu.make_async_copy(send_f.at[l], recv_f.at[me], r4).start()
        for c in tabs:
            c.wait()
        (w1h, w1l, w2h, w2l, w3h, w3l, w4h, w4l, tcr, tsr) = tab
        w1 = (w1h[...], w1l[...])
        w2 = (w2h[...], w2l[...])
        w3 = (w3h[...], w3l[...])
        w4 = (w4h[...], w4l[...])
        tc, ts = tcr[...], tsr[...]
        row = lax.broadcasted_iota(jnp.int32, (W, W), 0)
        col = lax.broadcasted_iota(jnp.int32, (W, W), 1)
        upper = col >= row
        half_row = lax.broadcasted_iota(jnp.int32, (64, W), 0)
        k = jnp.broadcast_to(mf[pl.ds(l, 1), :], (W, W))
        rolled = pltpu.roll(k, 0, 1, stride=1, stride_axis=0)
        k0 = split(jnp.where(upper, rolled, 0.0))
        k1 = split(jnp.where(upper, 0.0, rolled))

        pltpu.make_async_copy(recv, recv, r1).wait()

        @pl.when(hub)
        def _():
            for i in (4, 3, 5, 2, 6, 1, 7):
                signal(ready, me, lax.rem(z + i, 8))

        def forward(x):
            s = dot3(w1, split(x))
            parts = []
            for i in range(x.shape[1] // W):
                re, im = s[:W, i * W : (i + 1) * W], s[W:, i * W : (i + 1) * W]
                parts.append(jnp.concatenate([re * tc + im * ts, im * tc - re * ts], 1))
            return dot3(split(jnp.concatenate(parts, 0)), w2)

        def inverse(y):
            t = dot3(split(y), w3)
            parts = []
            for i in range(y.shape[0] // W):
                re, im = t[i * W : (i + 1) * W, :W], t[i * W : (i + 1) * W, W:]
                parts.append(jnp.concatenate([re * tc - im * ts, im * tc + re * ts], 0))
            return dot3(w4, split(jnp.concatenate(parts, 1)))

        pe, po = recv[:, 0, :], recv[:, 1, :]
        po_prev = jnp.where(half_row == 0, 0.0, pltpu.roll(po, 1, 0))
        p0 = split(jnp.concatenate([pe, po], 0))
        p1 = split(jnp.concatenate([po_prev, pe], 0))
        mixed = dot3(p0, k0) + dot3(p1, k1)
        conv_f = jnp.concatenate([recv[:, 2, :], recv[:, 3, :]], 0)
        f = forward(jnp.concatenate([mixed, conv_f], 1))
        mr, mi = f[:W, :W], f[:W, W:]
        cr, ci = f[W:, :W], f[W:, W:]
        glong = inverse(jnp.concatenate([cr * mr + ci * mi, ci * mr - cr * mi], 1)) * (N**-0.5)
        gls[:, 0, :] = glong[:64]
        gls[:, 1, :] = glong[64:]

        slot = z * 4 + l % 4

        def out_long():
            @pl.when(jnp.logical_not(hub))
            def _():
                pl.semaphore_wait(ready, 1)

            for dx, dy in OFFSETS:
                d = 2 * chip_at(dx, dy)
                out(gls.at[d], glr.at[slot], s3, r3, d, zo)
                if (dx, dy) != (0, 0):
                    out(gls.at[d + 1], glr.at[slot], s3, r3, d + 1, zo)

            @pl.when(jnp.logical_not(hub))
            def _():
                out(gls.at[me], glr.at[slot], s3, r3, me, zo)

            @pl.when(hub)
            def _():
                pltpu.make_async_copy(gls.at[me], glr.at[slot], r3).start()

        @pl.when(z >= zo)
        def _():
            out_long()

        pltpu.make_async_copy(recv_f, recv_f, r4).wait()
        h = forward(jnp.concatenate([recv_f[:, 0, :], recv_f[:, 1, :]], 0))
        hr, hi = h[:, :W], h[:, W:]
        both = inverse(
            jnp.concatenate(
                [
                    jnp.concatenate([mr * hr - mi * hi, mr * hi + mi * hr], 1),
                    jnp.concatenate([cr * hr + ci * hi, ci * hr - cr * hi], 1),
                ],
                0,
            )
        )
        recon, gmix = both[:, :W], both[:, W:]
        ge, gd = gmix[:64], gmix[64:]
        ge_next = jnp.where(half_row == 63, 0.0, pltpu.roll(ge, 63, 0))
        gms = split(gmix)
        gprod = dot3(gms, k0, NT) + dot3(split(jnp.concatenate([gd, ge_next], 0)), k1, NT)
        d = jnp.where(upper, dot3(p0, gms, TN), dot3(p1, gms, TN))
        for bit in range(7):
            moved = pltpu.roll(d, W - (1 << bit), 1)
            d = jnp.where((row >> bit) & 1 == 1, moved, d)
        gmid = jnp.sum(d, 0, keepdims=True) * (N**-0.5)

        ret[pl.ds(0, 64, stride=8), :] = recon[:64]
        ret[pl.ds(1, 64, stride=8), :] = recon[64:]
        ret[pl.ds(2, 64, stride=8), :] = gprod[:64]
        ret[pl.ds(3, 64, stride=8), :] = gprod[64:]
        for r in range(4, 8):
            ret[pl.ds(r, 64, stride=8), :] = jnp.broadcast_to(gmid, (64, W))

        for dx, dy in OFFSETS:
            d = 2 * chip_at(dx, dy)
            out(tile(ret, d), tile(back, l), s2, r2, d, z)
            if (dx, dy) != (0, 0):
                out(tile(ret, d + 1), tile(back, l), s2, r2, d + 1, z)
        pltpu.make_async_copy(tile(ret, me), tile(back, l), r2).start()

        @pl.when(z < zo)
        def _():
            out_long()

    def left(ref, count, sem):
        part = ref.at[pl.ds(0, count)]
        pltpu.make_async_copy(part, part, sem).wait()

    left(send, 31, s1)
    left(send_f, 31, s4)

    @pl.when(jnp.logical_not(works))
    def _():
        left(send, 1, s1)
        left(send_f, 1, s4)

    @pl.when(works)
    def _():
        left(gls, 63, s3)
        left(ret, 63 * 8, s2)

        @pl.when(jnp.logical_not(hub))
        def _():
            left(gls, 1, s3)

    pltpu.make_async_copy(back, back, r2).wait()

    def rows(r):
        return back[pl.ds(r, 32, stride=8), :]

    recon = jnp.concatenate([rows(0), rows(1)], 1)
    gprod = jnp.concatenate([rows(2), rows(3)], 1)
    go_o[...] = (go[...].astype(f32) * recon).astype(bf16)
    gi_o[...] = (gprod * va[...].astype(f32)).astype(bf16)
    gv_o[...] = (gprod * ig[...].astype(f32)).astype(bf16)
    gm_o[...] = rows(4)
    pltpu.make_async_copy(glr, glr, r3).wait()


def deliver(a, b, c, m, parts, a_o, b_o, c_o, gl_o, m_o, gl, sem):
    copies = [
        pltpu.make_async_copy(x, y, sem.at[i])
        for i, (x, y) in enumerate([(a, a_o), (b, b_o), (c, c_o), (m, m_o), (gl, gl_o)])
    ]
    for copy in copies[:4]:
        copy.start()
    total = parts[0:4]
    for i in range(1, 8):
        total = total + parts[4 * i : 4 * i + 4]
    gl[:, :W] = total[:, 0, :]
    gl[:, W:] = total[:, 1, :]
    copies[4].start()
    for copy in copies:
        copy.wait()


def local(outer_gate, inner_gate, values, grad_out, long_filter, mid_filter):
    tabs = tables()
    vm = pltpu.VMEM
    dma = pltpu.SemaphoreType.DMA
    hbm = pl.BlockSpec(memory_space=pl.ANY)
    vmem = pl.BlockSpec(memory_space=vm)
    ins = (outer_gate, inner_gate, values, grad_out, long_filter, mid_filter)
    outs = [((32, 256), bf16)] * 3 + [((32, W), f32)]
    shapes = [jax.ShapeDtypeStruct(*o) for o in outs]
    ins = [pltpu.with_memory_space_constraint(a, pltpu.HBM) for a in (*ins, *map(jnp.asarray, tabs))]
    results = pl.pallas_call(
        kernel,
        out_shape=[*[vm(*o) for o in outs], vm((32, 2, W), f32)],
        in_specs=[hbm] * 16,
        out_specs=[vmem] * 5,
        scratch_shapes=[
            *[vm((32, 256), bf16)] * 4,
            vm((32, 256), f32),
            vm((32, W), f32),
            *[vm(t.shape, t.dtype) for t in tabs],
            vm((32, 4, W), f32),
            vm((64, 4, W), f32),
            vm((32, 2, W), f32),
            vm((64, 2, W), f32),
            vm((64 * 8, W), f32),
            vm((32 * 8, W), f32),
            vm((64, 2, W), f32),
            dma((6,)),
            dma((10,)),
            *[dma] * 8,
            pltpu.SemaphoreType.REGULAR,
        ],
        compiler_params=pltpu.CompilerParams(
            collective_id=0, has_side_effects=True, vmem_limit_bytes=VMEM_BYTES
        ),
    )(*ins)
    return pl.pallas_call(
        deliver,
        out_shape=[*shapes[:3], jax.ShapeDtypeStruct((4, 256), f32), shapes[3]],
        in_specs=[vmem] * 5,
        out_specs=[hbm] * 5,
        scratch_shapes=[vm((4, 256), f32), dma((5,))],
        compiler_params=pltpu.CompilerParams(vmem_limit_bytes=VMEM_BYTES),
    )(*results)


def solution(mesh):
    in_specs = (
        P("ch", "ctx"),
        P("ch", "ctx"),
        P("ch", "ctx"),
        P("ch", "ctx"),
        P(None, "ctx"),
        P("ch", None),
    )
    out_specs = (P("ch", "ctx"), P("ch", "ctx"), P("ch", "ctx"), P("ch", "ctx"), P("ch", None))
    return jax.shard_map(local, mesh=mesh, in_specs=in_specs, out_specs=out_specs, check_vma=False)
```

```python
import functools
import math

import jax
import jax.numpy as jnp
import numpy as np
from jax import lax
from jax.experimental import pallas as pl
from jax.experimental.pallas import tpu as pltpu
from jax.sharding import PartitionSpec as P

MESH = pl.DeviceIdType.MESH
f32 = jnp.float32
bf16 = jnp.bfloat16
N = 16384
LEAD = 3
VMEM_BYTES = 16 * 1024 * 1024
W = 128


def split_np(a):
    a = np.asarray(a, np.float32)
    hi = a.astype(jnp.bfloat16)
    lo = (a - hi.astype(np.float32)).astype(jnp.bfloat16)
    return hi, lo


def tables():
    order = np.concatenate([np.arange(0, W, 2), np.arange(1, W, 2)]).astype(np.float64)
    k = np.arange(W, dtype=np.float64)
    ang = 2.0 * math.pi * (k + 0.5)[:, None] * order[None, :] / (2 * W)
    w1 = np.concatenate([np.cos(ang), -np.sin(ang)], 0)
    w1i = w1.T / N
    tw = 2.0 * math.pi * (k + 0.5)[:, None] * k[None, :] / (2 * N)
    tc, ts = np.cos(tw), np.sin(tw)
    a2 = 2.0 * math.pi * ((k[:, None] * k[None, :]) % W) / W
    c, s = np.cos(a2), np.sin(a2)
    w2 = np.block([[c, -s], [s, c]])
    (w1h, w1l), (w2h, w2l), (w3h, w3l), (w4h, w4l) = map(split_np, (w1, w2, w2.T, w1i))
    return (
        np.concatenate([w1h, w1h, w1l], 1),
        np.concatenate([w2h, w2h, w2l], 0),
        np.concatenate([w3h, w3h, w3l], 0),
        np.concatenate([w4h, w4h, w4l], 1),
        tc.astype(np.float32),
        ts.astype(np.float32),
    )


def split(a):
    hi = a.astype(bf16)
    lo = (a - hi.astype(f32)).astype(bf16)
    return hi, lo


def dot(a, b, dims=(((1,), (0,)), ((), ()))):
    return lax.dot_general(a, b, dims, preferred_element_type=f32)


def data(parts, axis):
    hi, lo = zip(*parts)
    return jnp.concatenate([*hi, *lo, *hi], axis)


def taps(parts, axis):
    hi, lo = zip(*parts)
    return jnp.concatenate([*hi, *hi, *lo], axis)


NT = (((1,), (1,)), ((), ()))
TN = (((0,), (0,)), ((), ()))


def ring(d, n):
    return min(d, n - d)


OFFSETS = sorted(
    [(dx, dy) for dx in range(4) for dy in range(8)], key=lambda o: -(ring(o[0], 4) + ring(o[1], 8))
)


def kernel(og_h, ig_h, va_h, go_h, lf_h, mf_h, *refs):
    tab_h = refs[:6]
    (go_o, gi_o, gv_o, gm_o, glr) = refs[6:11]
    (og, ig, va, go, lf, mf) = refs[11:17]
    tab = refs[17:23]
    (send, recv, send_f, recv_f, ret, back, gls) = refs[23:30]
    (in_sem, tab_sem, s1, r1, s2, r2, s3, r3, s4, r4, ready, here, near, far) = refs[30:]

    me = lax.axis_index("ctx")
    z = lax.axis_index("ch")
    chip = me // 2
    core = me % 2
    px, py = chip // 8, chip % 8

    def channel(c):
        x, y = c // 8, c % 8
        return jnp.where(y < LEAD, LEAD * x + y, (8 - LEAD) * x + y + 3 * LEAD)

    works = core == 1
    leads = py < LEAD
    l = channel(chip)
    zo = l // 4
    hub = z == zo
    told = jnp.logical_and(zo < LEAD, z >= 4)
    bar = pltpu.get_barrier_semaphore()

    def signal(sem, ctx, ch):
        pl.semaphore_signal(sem, inc=1, device_id=(ctx, ch), device_id_type=MESH)

    def chip_at(dx, dy):
        return lax.rem(px + dx, 4) * 8 + lax.rem(py + dy, 8)

    ins = [
        pltpu.make_async_copy(a, b, in_sem.at[i])
        for i, (a, b) in enumerate(
            [(ig_h, ig), (va_h, va), (go_h, go), (og_h, og), (lf_h, lf), (mf_h, mf)]
        )
    ]
    for c in ins:
        c.start()
    tabs = [pltpu.make_async_copy(a, b, tab_sem.at[i]) for i, (a, b) in enumerate(zip(tab_h, tab))]

    @pl.when(core == 0)
    def _():
        signal(bar, me + 1, z)

    @pl.when(z < LEAD)
    def _():
        for p in (4, 5, 6, 7):
            for i in range(4):
                g = 4 * z + i
                signal(bar, 2 * ((g // LEAD) * 8 + g % LEAD) + 1, p)

    @pl.when(works)
    def _():
        for dx, dy in OFFSETS[:-1]:
            signal(bar, 2 * chip_at(dx, dy) + jnp.where(leads, 1, 0), z)

        @pl.when(jnp.logical_not(leads))
        def _():
            signal(bar, me - 1, z)

        @pl.when(z < zo)
        def _():
            signal(bar, me, zo)

        @pl.when(hub)
        def _():
            for p in range(1, 8):
                above = z < p if p < 4 else jnp.logical_and(z < p, z >= LEAD)

                @pl.when(above)
                def _():
                    signal(bar, me, p)

        for c in tabs:
            c.start()

    for c in ins:
        c.wait()

    product = ig[...].astype(f32) * va[...].astype(f32)
    conv = go[...].astype(f32) * og[...].astype(f32)
    filt = lf[...]
    send[:, 0, :] = product[:, :W]
    send[:, 1, :] = product[:, W:]
    send[:, 2, :] = conv[:, :W]
    send[:, 3, :] = conv[:, W:]
    send_f[:, 0, :] = filt[:, :W]
    send_f[:, 1, :] = filt[:, W:]

    def out(src, dst, ssem, rsem, d, p):
        pltpu.make_async_remote_copy(
            src_ref=src,
            dst_ref=dst,
            send_sem=ssem,
            recv_sem=rsem,
            device_id=(d, p),
            device_id_type=MESH,
        ).start()

    def put_all(src, dst, ssem, rsem, lead):
        def put(c):
            out(src.at[channel(c)], dst.at[me], ssem, rsem, 2 * c + 1, z)

        for off in OFFSETS:
            c = chip_at(*off)
            mine = (c % 8 < LEAD) == lead
            if off == (0, 0):
                mine = jnp.logical_and(mine, core == 0)
            pl.when(mine)(functools.partial(put, c))

    @pl.when(works)
    def _():
        from_below = jnp.where(hub, zo, jnp.where(z > zo, jnp.where(told, 64, 1), 0))
        pl.semaphore_wait(bar, 4 * LEAD + 1 - jnp.where(leads, 1, 0) + from_below)
        signal(near, me - 1, z)

        @pl.when(jnp.logical_and(z > zo, jnp.logical_not(told)))
        def _():
            signal(here, me, zo)

    @pl.when(core == 0)
    def _():
        pl.semaphore_wait(near, 1)

    put_all(send, recv, s1, r1, True)

    @pl.when(core == 0)
    def _():
        pl.semaphore_wait(bar, 32 - 4 * LEAD)
        signal(far, me + 1, z)

    @pl.when(works)
    def _():
        pl.semaphore_wait(far, 1)

    put_all(send, recv, s1, r1, False)
    put_all(send_f, recv_f, s4, r4, True)
    put_all(send_f, recv_f, s4, r4, False)

    @pl.when(works)
    def _():
        pltpu.make_async_copy(send.at[l], recv.at[me], r1).start()
        pltpu.make_async_copy(send_f.at[l], recv_f.at[me], r4).start()

        for c in tabs:
            c.wait()
        (w1, w2, w3, w4, tcr, tsr) = tab
        tc, ts = tcr[...], tsr[...]
        row = lax.broadcasted_iota(jnp.int32, (W, W), 0)
        col = lax.broadcasted_iota(jnp.int32, (W, W), 1)
        upper = col >= row
        half_row = lax.broadcasted_iota(jnp.int32, (64, W), 0)
        k = jnp.broadcast_to(mf[pl.ds(l, 1), :], (W, W))
        rolled = pltpu.roll(k, 0, 1, stride=1, stride_axis=0)
        k0 = split(jnp.where(upper, rolled, 0.0))
        k1 = split(jnp.where(upper, 0.0, rolled))

        pltpu.make_async_copy(recv, recv, r1).wait()

        @pl.when(hub)
        def _():
            for p in range(7):
                @pl.when(p < z)
                def _():
                    signal(ready, me, p)

        def ready_above():
            top = jnp.where(zo < LEAD, 3, 7)

            @pl.when(z < top)
            def _():
                pl.semaphore_wait(here, top - z)

            for p in range(7, 0, -1):
                @pl.when(jnp.logical_and(z < p, p <= top))
                def _():
                    signal(ready, me, p)

        def forward(x):
            s = dot(w1[...], data([split(x)], 0))
            re, im = s[:W], s[W:]
            t = jnp.concatenate([re * tc + im * ts, im * tc - re * ts], 1)
            t = dot(data([split(t)], 1), w2[...])
            return t[:, :W], t[:, W:]

        def inverse(y):
            t = dot(data([split(y)], 1), w3[...])
            parts = []
            for i in range(y.shape[0] // W):
                re, im = t[i * W : (i + 1) * W, :W], t[i * W : (i + 1) * W, W:]
                parts.append(jnp.concatenate([re * tc - im * ts, im * tc + re * ts], 0))
            return dot(w4[...], data([split(jnp.concatenate(parts, 1))], 0))

        def times(a, b):
            return jnp.concatenate([a[0] * b[0] - a[1] * b[1], a[0] * b[1] + a[1] * b[0]], 1)

        def times_conj(a, b):
            return jnp.concatenate([a[0] * b[0] + a[1] * b[1], a[1] * b[0] - a[0] * b[1]], 1)

        c = forward(jnp.concatenate([recv[:, 2, :], recv[:, 3, :]], 0))
        pe, po = recv[:, 0, :], recv[:, 1, :]
        po_prev = jnp.where(half_row == 0, 0.0, pltpu.roll(po, 1, 0))
        p0 = split(jnp.concatenate([pe, po], 0))
        p1 = split(jnp.concatenate([po_prev, pe], 0))
        m = forward(dot(data([p0, p1], 1), taps([k0, k1], 0)))
        glong = inverse(times_conj(c, m)) * (N**-0.5)
        gls[:, 0, :] = glong[:64]
        gls[:, 1, :] = glong[64:]

        slot = z * 4 + l % 4

        def out_long():
            @pl.when(jnp.logical_not(jnp.logical_or(hub, told)))
            def _():
                pl.semaphore_wait(ready, 1)

            for dx, dy in OFFSETS:
                d = 2 * chip_at(dx, dy)
                out(gls.at[d + 1 - core], glr.at[slot], s3, r3, d + 1 - core, zo)
                if (dx, dy) != (0, 0):
                    out(gls.at[d + core], glr.at[slot], s3, r3, d + core, zo)

            @pl.when(jnp.logical_not(hub))
            def _():
                out(gls.at[me], glr.at[slot], s3, r3, me, zo)

            @pl.when(hub)
            def _():
                pltpu.make_async_copy(gls.at[me], glr.at[slot], r3).start()

        @pl.when(z >= zo)
        def _():
            @pl.when(jnp.logical_and(hub, zo >= LEAD))
            def _():
                ready_above()

            out_long()

            @pl.when(jnp.logical_and(hub, zo < LEAD))
            def _():
                ready_above()

        pltpu.make_async_copy(recv_f, recv_f, r4).wait()
        h = forward(jnp.concatenate([recv_f[:, 0, :], recv_f[:, 1, :]], 0))
        both = inverse(jnp.concatenate([times(m, h), times_conj(c, h)], 0))
        recon, gmix = both[:, :W], both[:, W:]
        ge, gd = gmix[:64], gmix[64:]
        ge_next = jnp.where(half_row == 63, 0.0, pltpu.roll(ge, 63, 0))
        g0 = split(gmix)
        g1 = split(jnp.concatenate([gd, ge_next], 0))
        gprod = dot(data([g0, g1], 1), taps([k0, k1], 1), NT)
        g3 = taps([g0], 0)
        d = jnp.where(upper, dot(data([p0], 0), g3, TN), dot(data([p1], 0), g3, TN))
        for bit in range(7):
            moved = pltpu.roll(d, W - (1 << bit), 1)
            d = jnp.where((row >> bit) & 1 == 1, moved, d)
        gmid = jnp.sum(d, 0, keepdims=True) * (N**-0.5)

        ret[:, 0, :] = recon[:64]
        ret[:, 1, :] = recon[64:]
        ret[:, 2, :] = gprod[:64]
        ret[:, 3, :] = gprod[64:]
        ret[:, 4, :] = jnp.broadcast_to(gmid, (64, W))

        for dx, dy in OFFSETS:
            d = 2 * chip_at(dx, dy)
            out(ret.at[d + 1 - core], back.at[l], s2, r2, d + 1 - core, z)
            if (dx, dy) != (0, 0):
                out(ret.at[d + core], back.at[l], s2, r2, d + core, z)
        pltpu.make_async_copy(ret.at[me], back.at[l], r2).start()

        @pl.when(z < zo)
        def _():
            out_long()

    def left(ref, count, sem):
        part = ref.at[pl.ds(0, count)]
        pltpu.make_async_copy(part, part, sem).wait()

    left(send, 31, s1)
    left(send_f, 31, s4)

    @pl.when(jnp.logical_not(works))
    def _():
        left(send, 1, s1)
        left(send_f, 1, s4)

    @pl.when(works)
    def _():
        left(gls, 63, s3)
        left(ret, 63, s2)

        @pl.when(jnp.logical_not(hub))
        def _():
            left(gls, 1, s3)

    pltpu.make_async_copy(back, back, r2).wait()
    recon = jnp.concatenate([back[:, 0, :], back[:, 1, :]], 1)
    gprod = jnp.concatenate([back[:, 2, :], back[:, 3, :]], 1)
    go_o[...] = (go[...].astype(f32) * recon).astype(bf16)
    gi_o[...] = (gprod * va[...].astype(f32)).astype(bf16)
    gv_o[...] = (gprod * ig[...].astype(f32)).astype(bf16)
    gm_o[...] = back[:, 4, :]
    pltpu.make_async_copy(glr, glr, r3).wait()


def deliver(a, b, c, m, parts, a_o, b_o, c_o, gl_o, m_o, gl, sem):
    copies = [
        pltpu.make_async_copy(x, y, sem.at[i])
        for i, (x, y) in enumerate([(a, a_o), (b, b_o), (c, c_o), (m, m_o), (gl, gl_o)])
    ]
    for copy in copies[:4]:
        copy.start()
    total = parts[0:4]
    for i in range(1, 8):
        total = total + parts[4 * i : 4 * i + 4]
    gl[:, :W] = total[:, 0, :]
    gl[:, W:] = total[:, 1, :]
    copies[4].start()
    for copy in copies:
        copy.wait()


def local(outer_gate, inner_gate, values, grad_out, long_filter, mid_filter):
    tabs = tables()
    vm = pltpu.VMEM
    dma = pltpu.SemaphoreType.DMA
    hbm = pl.BlockSpec(memory_space=pl.ANY)
    vmem = pl.BlockSpec(memory_space=vm)
    ins = (outer_gate, inner_gate, values, grad_out, long_filter, mid_filter)
    outs = [((32, 256), bf16)] * 3 + [((32, W), f32)]
    shapes = [jax.ShapeDtypeStruct(*o) for o in outs]
    ins = [pltpu.with_memory_space_constraint(a, pltpu.HBM) for a in (*ins, *map(jnp.asarray, tabs))]
    results = pl.pallas_call(
        kernel,
        out_shape=[*[vm(*o) for o in outs], vm((32, 2, W), f32)],
        in_specs=[hbm] * 12,
        out_specs=[vmem] * 5,
        scratch_shapes=[
            *[vm((32, 256), bf16)] * 4,
            vm((32, 256), f32),
            vm((32, W), f32),
            *[vm(t.shape, t.dtype) for t in tabs],
            vm((32, 4, W), f32),
            vm((64, 4, W), f32),
            vm((32, 2, W), f32),
            vm((64, 2, W), f32),
            vm((64, 5, W), f32),
            vm((32, 5, W), f32),
            vm((64, 2, W), f32),
            dma((6,)),
            dma((6,)),
            *[dma] * 8,
            *[pltpu.SemaphoreType.REGULAR] * 4,
        ],
        compiler_params=pltpu.CompilerParams(
            collective_id=0, has_side_effects=True, vmem_limit_bytes=VMEM_BYTES
        ),
    )(*ins)
    return pl.pallas_call(
        deliver,
        out_shape=[*shapes[:3], jax.ShapeDtypeStruct((4, 256), f32), shapes[3]],
        in_specs=[vmem] * 5,
        out_specs=[hbm] * 5,
        scratch_shapes=[vm((4, 256), f32), dma((5,))],
        compiler_params=pltpu.CompilerParams(vmem_limit_bytes=VMEM_BYTES),
    )(*results)


def solution(mesh):
    in_specs = (
        P("ch", "ctx"),
        P("ch", "ctx"),
        P("ch", "ctx"),
        P("ch", "ctx"),
        P(None, "ctx"),
        P("ch", None),
    )
    out_specs = (P("ch", "ctx"), P("ch", "ctx"), P("ch", "ctx"), P("ch", "ctx"), P("ch", None))
    return jax.shard_map(local, mesh=mesh, in_specs=in_specs, out_specs=out_specs, check_vma=False)
```

```python
import functools
import math

import jax
import jax.numpy as jnp
import numpy as np
from jax import lax
from jax.experimental import pallas as pl
from jax.experimental.pallas import tpu as pltpu
from jax.sharding import PartitionSpec as P

MESH = pl.DeviceIdType.MESH
f32 = jnp.float32
bf16 = jnp.bfloat16
N = 16384
LEAD = 12
DIRECT = 2
TOLD = 4
VMEM_BYTES = 16 * 1024 * 1024
W = 128


def split_np(a):
    a = np.asarray(a, np.float32)
    hi = a.astype(jnp.bfloat16)
    lo = (a - hi.astype(np.float32)).astype(jnp.bfloat16)
    return hi, lo


def tables():
    order = np.concatenate([np.arange(0, W, 2), np.arange(1, W, 2)]).astype(np.float64)
    k = np.arange(W, dtype=np.float64)
    ang = 2.0 * math.pi * (k + 0.5)[:, None] * order[None, :] / (2 * W)
    w1 = np.concatenate([np.cos(ang), -np.sin(ang)], 0)
    w1i = w1.T / N
    tw = 2.0 * math.pi * (k + 0.5)[:, None] * k[None, :] / (2 * N)
    tc, ts = np.cos(tw), np.sin(tw)
    a2 = 2.0 * math.pi * ((k[:, None] * k[None, :]) % W) / W
    c, s = np.cos(a2), np.sin(a2)
    w2 = np.block([[c, -s], [s, c]])
    (w1h, w1l), (w2h, w2l), (w3h, w3l), (w4h, w4l) = map(split_np, (w1, w2, w2.T, w1i))
    return (
        np.concatenate([w1h, w1h, w1l], 1),
        np.concatenate([w2h, w2h, w2l], 0),
        np.concatenate([w3h, w3h, w3l], 0),
        np.concatenate([w4h, w4h, w4l], 1),
        tc.astype(np.float32),
        ts.astype(np.float32),
    )


def split(a):
    hi = a.astype(bf16)
    lo = (a - hi.astype(f32)).astype(bf16)
    return hi, lo


def dot(a, b, dims=(((1,), (0,)), ((), ()))):
    return lax.dot_general(a, b, dims, preferred_element_type=f32)


def data(parts, axis):
    hi, lo = zip(*parts)
    return jnp.concatenate([*hi, *lo, *hi], axis)


def taps(parts, axis):
    hi, lo = zip(*parts)
    return jnp.concatenate([*hi, *hi, *lo], axis)


NT = (((1,), (1,)), ((), ()))
TN = (((0,), (0,)), ((), ()))


def ring(d, n):
    return min(d, n - d)


OFFSETS = sorted(
    [(dx, dy) for dx in range(4) for dy in range(8)], key=lambda o: -(ring(o[0], 4) + ring(o[1], 8))
)


CHIPS = [x * 8 + y for x, y in reversed(OFFSETS)]


PLACES = [
    *[(0, 0), (0, 1), (1, 0), (3, 0)],
    *[(1, 1), (3, 1), (2, 0), (2, 1)],
    *[(0, 7), (0, 2), (1, 2), (0, 3)],
    *[(1, 7), (3, 7), (0, 6), (3, 2)],
    *[(0, 5), (0, 4), (2, 5), (2, 4)],
    *[(3, 6), (3, 3), (2, 6), (3, 4)],
    *[(1, 6), (1, 3), (3, 5), (1, 4)],
    *[(2, 7), (2, 2), (1, 5), (2, 3)],
]


def pick(i, values):
    if len(values) == 1:
        return values[0]
    half = len(values) // 2
    return jnp.where(i < half, pick(i, values[:half]), pick(i - half, values[half:]))


def kernel(og_h, ig_h, va_h, go_h, lf_h, mf_h, *refs):
    tab_h = refs[:6]
    (go_o, gi_o, gv_o, gm_o, glr) = refs[6:11]
    (og, ig, va, go, lf, mf) = refs[11:17]
    tab = refs[17:23]
    (send, recv, send_f, recv_f, ret, back, gls) = refs[23:30]
    (in_sem, tab_sem, s1, r1, s2, r2, s3, r3, s4, r4, ready, here, near, far) = refs[30:]

    me = lax.axis_index("ctx")
    z = lax.axis_index("ch")
    chip = me // 2
    core = me % 2
    px, py = chip // 8, chip % 8

    def channel(x, y):
        return pick(x, [PLACES.index((i, y)) for i in range(4)])

    works = core == 1
    l = pick(py, [channel(px, y) for y in range(8)])
    leads = l < LEAD
    zo = l // 4
    hub = z == zo
    told = jnp.logical_and(zo < TOLD, z >= TOLD)
    bar = pltpu.get_barrier_semaphore()

    def signal(sem, ctx, ch):
        pl.semaphore_signal(sem, inc=1, device_id=(ctx, ch), device_id_type=MESH)

    def chip_at(dx, dy):
        return lax.rem(px + dx, 4) * 8 + lax.rem(py + dy, 8)

    @pl.when(core == 0)
    def _():
        signal(bar, me + 1, z)

    @pl.when(works)
    def _():
        for dx, dy in OFFSETS[:-1]:
            signal(bar, 2 * chip_at(dx, dy) + jnp.where(leads, 1, 0), z)

        @pl.when(jnp.logical_not(leads))
        def _():
            signal(bar, me - 1, z)

        @pl.when(z < zo)
        def _():
            signal(bar, me, zo)

        @pl.when(hub)
        def _():
            for p in range(1, 8):
                above = z < p if p < TOLD else jnp.logical_and(z < p, z >= TOLD)

                @pl.when(above)
                def _():
                    signal(bar, me, p)


    ins = [
        pltpu.make_async_copy(a, b, in_sem.at[i])
        for i, (a, b) in enumerate(
            [(ig_h, ig), (va_h, va), (go_h, go), (og_h, og), (lf_h, lf), (mf_h, mf)]
        )
    ]
    for c in ins:
        c.start()
    tabs = [pltpu.make_async_copy(a, b, tab_sem.at[i]) for i, (a, b) in enumerate(zip(tab_h, tab))]

    @pl.when(z < TOLD)
    def _():
        for p in range(TOLD, 8):
            for i in range(4):
                at = [PLACES[4 * q + i] for q in range(TOLD)]
                signal(bar, pick(z, [2 * (8 * x + y) + (1 if q < DIRECT else 0) for q, (x, y) in enumerate(at)]), p)

    @pl.when(works)
    def _():
        for c in tabs:
            c.start()

    for c in ins[:4]:
        c.wait()

    product = ig[...].astype(f32) * va[...].astype(f32)
    conv = go[...].astype(f32) * og[...].astype(f32)
    send[:, 0, :] = product[:, :W]
    send[:, 1, :] = product[:, W:]
    send[:, 2, :] = conv[:, :W]
    send[:, 3, :] = conv[:, W:]

    @pl.when(works)
    def _():
        from_below = jnp.where(hub, zo, jnp.where(z > zo, jnp.where(told, jnp.where(zo < DIRECT, 64, 0), 1), 0))
        pl.semaphore_wait(bar, LEAD + 1 - jnp.where(leads, 1, 0) + from_below)
        signal(near, me - 1, z)

        @pl.when(jnp.logical_and(z > zo, jnp.logical_not(told)))
        def _():
            signal(here, me, zo)

    def out(src, dst, ssem, rsem, d, p):
        pltpu.make_async_remote_copy(
            src_ref=src,
            dst_ref=dst,
            send_sem=ssem,
            recv_sem=rsem,
            device_id=(d, p),
            device_id_type=MESH,
        ).start()

    def put_all(src, dst, ssem, rsem, channels):
        def put(x, y):
            out(src.at[channel(x, y)], dst.at[me], ssem, rsem, 2 * (8 * x + y) + 1, z)

        def put_near(x, y):
            mine = jnp.logical_and(works, jnp.logical_and(px == x, py == y))
            pl.when(jnp.logical_not(mine))(functools.partial(put, x, y))

        chips = [PLACES[i] for i in channels]
        rows = [y for y in range(8) if all((x, y) in chips for x in range(4))]
        for dx in (2, 1, 3):
            for y in rows:
                put(lax.rem(px + dx, 4), y)
        for y in rows:
            put_near(px, y)
        for x, y in chips:
            if y not in rows:
                put_near(x, y)

    @pl.when(core == 0)
    def _():
        pl.semaphore_wait(near, 1)

    put_all(send, recv, s1, r1, range(LEAD))

    @pl.when(core == 0)
    def _():
        pl.semaphore_wait(bar, 32 - LEAD + jnp.where(jnp.logical_and(told, zo >= DIRECT), 64, 0))
        signal(far, me + 1, z)

    @pl.when(works)
    def _():
        pl.semaphore_wait(far, 1)

    put_all(send, recv, s1, r1, range(LEAD, 32))
    for c in ins[4:]:
        c.wait()
    filt = lf[...]
    send_f[:, 0, :] = filt[:, :W]
    send_f[:, 1, :] = filt[:, W:]
    put_all(send_f, recv_f, s4, r4, range(32))

    @pl.when(works)
    def _():
        pltpu.make_async_copy(send.at[l], recv.at[me], r1).start()
        pltpu.make_async_copy(send_f.at[l], recv_f.at[me], r4).start()

        for c in tabs:
            c.wait()
        (w1, w2, w3, w4, tcr, tsr) = tab
        tc, ts = tcr[...], tsr[...]
        row = lax.broadcasted_iota(jnp.int32, (W, W), 0)
        col = lax.broadcasted_iota(jnp.int32, (W, W), 1)
        upper = col >= row
        half_row = lax.broadcasted_iota(jnp.int32, (64, W), 0)
        k = jnp.broadcast_to(mf[pl.ds(l, 1), :], (W, W))
        rolled = pltpu.roll(k, 0, 1, stride=1, stride_axis=0)
        k0 = split(jnp.where(upper, rolled, 0.0))
        k1 = split(jnp.where(upper, 0.0, rolled))

        pltpu.make_async_copy(recv, recv, r1).wait()

        @pl.when(hub)
        def _():
            for p in range(7):
                @pl.when(p < z)
                def _():
                    signal(ready, me, p)

        def ready_above():
            top = jnp.where(zo < TOLD, TOLD - 1, 7)

            @pl.when(z < top)
            def _():
                pl.semaphore_wait(here, top - z)

            for p in range(7, 0, -1):
                @pl.when(jnp.logical_and(z < p, p <= top))
                def _():
                    signal(ready, me, p)

        pl.when(jnp.logical_and(hub, zo >= TOLD))(ready_above)

        def forward(x):
            s = dot(w1[...], data([split(x)], 0))
            re, im = s[:W], s[W:]
            t = jnp.concatenate([re * tc + im * ts, im * tc - re * ts], 1)
            t = dot(data([split(t)], 1), w2[...])
            return t[:, :W], t[:, W:]

        def inverse(y):
            t = dot(data([split(y)], 1), w3[...])
            parts = []
            for i in range(y.shape[0] // W):
                re, im = t[i * W : (i + 1) * W, :W], t[i * W : (i + 1) * W, W:]
                parts.append(jnp.concatenate([re * tc - im * ts, im * tc + re * ts], 0))
            return dot(w4[...], data([split(jnp.concatenate(parts, 1))], 0))

        def times(a, b):
            return jnp.concatenate([a[0] * b[0] - a[1] * b[1], a[0] * b[1] + a[1] * b[0]], 1)

        def times_conj(a, b):
            return jnp.concatenate([a[0] * b[0] + a[1] * b[1], a[1] * b[0] - a[0] * b[1]], 1)

        c = forward(jnp.concatenate([recv[:, 2, :], recv[:, 3, :]], 0))
        pe, po = recv[:, 0, :], recv[:, 1, :]
        po_prev = jnp.where(half_row == 0, 0.0, pltpu.roll(po, 1, 0))
        p0 = split(jnp.concatenate([pe, po], 0))
        p1 = split(jnp.concatenate([po_prev, pe], 0))
        m = forward(dot(data([p0, p1], 1), taps([k0, k1], 0)))
        slot = z * 4 + l % 4

        def long_gradient():
            glong = inverse(times_conj(c, m)) * (N**-0.5)
            gls[:, 0, :] = glong[:64]
            gls[:, 1, :] = glong[64:]

            @pl.when(jnp.logical_not(jnp.logical_or(hub, told)))
            def _():
                pl.semaphore_wait(ready, 1)

            def put(d):
                out(gls.at[d], glr.at[slot], s3, r3, d, zo)

            for i in CHIPS:
                put(2 * i + 1 - core)
                pl.when(jnp.logical_not(jnp.logical_and(hub, chip == i)))(
                    functools.partial(put, 2 * i + core)
                )

            @pl.when(hub)
            def _():
                pltpu.make_async_copy(gls.at[me], glr.at[slot], r3).start()

        soon = jnp.logical_and(z >= zo, z >= 3)
        pl.when(soon)(long_gradient)

        pltpu.make_async_copy(recv_f, recv_f, r4).wait()
        h = forward(jnp.concatenate([recv_f[:, 0, :], recv_f[:, 1, :]], 0))
        both = inverse(jnp.concatenate([times(m, h), times_conj(c, h)], 0))
        recon, gmix = both[:, :W], both[:, W:]
        ge, gd = gmix[:64], gmix[64:]
        ge_next = jnp.where(half_row == 63, 0.0, pltpu.roll(ge, 63, 0))
        g0 = split(gmix)
        g1 = split(jnp.concatenate([gd, ge_next], 0))
        gprod = dot(data([g0, g1], 1), taps([k0, k1], 1), NT)
        g3 = taps([g0], 0)
        d = jnp.where(upper, dot(data([p0], 0), g3, TN), dot(data([p1], 0), g3, TN))
        for bit in range(7):
            moved = pltpu.roll(d, W - (1 << bit), 1)
            d = jnp.where((row >> bit) & 1 == 1, moved, d)
        gmid = jnp.sum(d, 0, keepdims=True) * (N**-0.5)

        ret[:, 0, :] = recon[:64]
        ret[:, 1, :] = recon[64:]
        ret[:, 2, :] = gprod[:64]
        ret[:, 3, :] = gprod[64:]
        ret[:, 4, :] = jnp.broadcast_to(gmid, (64, W))

        def put_back(d):
            out(ret.at[d], back.at[l], s2, r2, d, z)

        for i in CHIPS:
            put_back(2 * i + 1 - core)
            pl.when(chip != i)(functools.partial(put_back, 2 * i + core))
        pltpu.make_async_copy(ret.at[me], back.at[l], r2).start()

        pl.when(jnp.logical_and(hub, zo < TOLD))(ready_above)
        pl.when(jnp.logical_not(soon))(long_gradient)

    def left(ref, count, sem):
        part = ref.at[pl.ds(0, count)]
        pltpu.make_async_copy(part, part, sem).wait()

    left(send, 31, s1)
    left(send_f, 31, s4)

    @pl.when(jnp.logical_not(works))
    def _():
        left(send, 1, s1)
        left(send_f, 1, s4)

    @pl.when(works)
    def _():
        left(gls, 63, s3)
        left(ret, 63, s2)

        @pl.when(jnp.logical_not(hub))
        def _():
            left(gls, 1, s3)

    pltpu.make_async_copy(back, back, r2).wait()
    recon = jnp.concatenate([back[:, 0, :], back[:, 1, :]], 1)
    gprod = jnp.concatenate([back[:, 2, :], back[:, 3, :]], 1)
    go_o[...] = (go[...].astype(f32) * recon).astype(bf16)
    gi_o[...] = (gprod * va[...].astype(f32)).astype(bf16)
    gv_o[...] = (gprod * ig[...].astype(f32)).astype(bf16)
    gm_o[...] = back[:, 4, :]
    pltpu.make_async_copy(glr, glr, r3).wait()


def deliver(a, b, c, m, parts, a_o, b_o, c_o, gl_o, m_o, gl, sem):
    copies = [
        pltpu.make_async_copy(x, y, sem.at[i])
        for i, (x, y) in enumerate([(a, a_o), (b, b_o), (c, c_o), (m, m_o), (gl, gl_o)])
    ]
    for copy in copies[:4]:
        copy.start()
    total = parts[0:4]
    for i in range(1, 8):
        total = total + parts[4 * i : 4 * i + 4]
    gl[:, :W] = total[:, 0, :]
    gl[:, W:] = total[:, 1, :]
    copies[4].start()
    for copy in copies:
        copy.wait()


def local(outer_gate, inner_gate, values, grad_out, long_filter, mid_filter):
    tabs = tables()
    vm = pltpu.VMEM
    dma = pltpu.SemaphoreType.DMA
    hbm = pl.BlockSpec(memory_space=pl.ANY)
    vmem = pl.BlockSpec(memory_space=vm)
    ins = (outer_gate, inner_gate, values, grad_out, long_filter, mid_filter)
    outs = [((32, 256), bf16)] * 3 + [((32, W), f32)]
    shapes = [jax.ShapeDtypeStruct(*o) for o in outs]
    ins = [pltpu.with_memory_space_constraint(a, pltpu.HBM) for a in (*ins, *map(jnp.asarray, tabs))]
    results = pl.pallas_call(
        kernel,
        out_shape=[*[vm(*o) for o in outs], vm((32, 2, W), f32)],
        in_specs=[hbm] * 12,
        out_specs=[vmem] * 5,
        scratch_shapes=[
            *[vm((32, 256), bf16)] * 4,
            vm((32, 256), f32),
            vm((32, W), f32),
            *[vm(t.shape, t.dtype) for t in tabs],
            vm((32, 4, W), f32),
            vm((64, 4, W), f32),
            vm((32, 2, W), f32),
            vm((64, 2, W), f32),
            vm((64, 5, W), f32),
            vm((32, 5, W), f32),
            vm((64, 2, W), f32),
            dma((6,)),
            dma((6,)),
            *[dma] * 8,
            *[pltpu.SemaphoreType.REGULAR] * 4,
        ],
        compiler_params=pltpu.CompilerParams(
            collective_id=0, has_side_effects=True, vmem_limit_bytes=VMEM_BYTES
        ),
    )(*ins)
    return pl.pallas_call(
        deliver,
        out_shape=[*shapes[:3], jax.ShapeDtypeStruct((4, 256), f32), shapes[3]],
        in_specs=[vmem] * 5,
        out_specs=[hbm] * 5,
        scratch_shapes=[vm((4, 256), f32), dma((5,))],
        compiler_params=pltpu.CompilerParams(vmem_limit_bytes=VMEM_BYTES),
    )(*results)


def solution(mesh):
    in_specs = (
        P("ch", "ctx"),
        P("ch", "ctx"),
        P("ch", "ctx"),
        P("ch", "ctx"),
        P(None, "ctx"),
        P("ch", None),
    )
    out_specs = (P("ch", "ctx"), P("ch", "ctx"), P("ch", "ctx"), P("ch", "ctx"), P("ch", None))
    return jax.shard_map(local, mesh=mesh, in_specs=in_specs, out_specs=out_specs, check_vma=False)
```

```python
import functools
import math

import jax
import jax.numpy as jnp
import numpy as np
from jax import lax
from jax.experimental import pallas as pl
from jax.experimental.pallas import tpu as pltpu
from jax.sharding import PartitionSpec as P

MESH = pl.DeviceIdType.MESH
f32 = jnp.float32
bf16 = jnp.bfloat16
N = 16384
LEAD = 12
DIRECT = 0
TOLD = 4
VMEM_BYTES = 16 * 1024 * 1024
W = 128


def split_np(a):
    a = np.asarray(a, np.float32)
    hi = a.astype(jnp.bfloat16)
    lo = (a - hi.astype(np.float32)).astype(jnp.bfloat16)
    return hi, lo


def tables():
    order = np.concatenate([np.arange(0, W, 2), np.arange(1, W, 2)]).astype(np.float64)
    k = np.arange(W, dtype=np.float64)
    ang = 2.0 * math.pi * (k + 0.5)[:, None] * order[None, :] / (2 * W)
    w1 = np.concatenate([np.cos(ang), -np.sin(ang)], 0)
    w1i = w1.T / N
    tw = 2.0 * math.pi * (k + 0.5)[:, None] * k[None, :] / (2 * N)
    tc, ts = np.cos(tw), np.sin(tw)
    a2 = 2.0 * math.pi * ((k[:, None] * k[None, :]) % W) / W
    c, s = np.cos(a2), np.sin(a2)
    w2 = np.block([[c, -s], [s, c]])
    (w1h, w1l), (w2h, w2l), (w3h, w3l), (w4h, w4l) = map(split_np, (w1, w2, w2.T, w1i))
    return (
        np.concatenate([w1h, w1h, w1l], 1),
        np.concatenate([w2h, w2h, w2l], 0),
        np.concatenate([w3h, w3h, w3l], 0),
        np.concatenate([w4h, w4h, w4l], 1),
        tc.astype(np.float32),
        ts.astype(np.float32),
    )


def split(a):
    hi = a.astype(bf16)
    lo = (a - hi.astype(f32)).astype(bf16)
    return hi, lo


def dot(a, b, dims=(((1,), (0,)), ((), ()))):
    return lax.dot_general(a, b, dims, preferred_element_type=f32)


def data(parts, axis):
    hi, lo = zip(*parts)
    return jnp.concatenate([*hi, *lo, *hi], axis)


def taps(parts, axis):
    hi, lo = zip(*parts)
    return jnp.concatenate([*hi, *hi, *lo], axis)


NT = (((1,), (1,)), ((), ()))
TN = (((0,), (0,)), ((), ()))


def ring(d, n):
    return min(d, n - d)


OFFSETS = sorted(
    [(dx, dy) for dx in range(4) for dy in range(8)], key=lambda o: -(ring(o[0], 4) + ring(o[1], 8))
)


CHIPS = [x * 8 + y for x, y in reversed(OFFSETS)]


PLACES = [
    *[(0, 0), (0, 1), (1, 0), (3, 0)],
    *[(1, 1), (3, 1), (2, 0), (2, 1)],
    *[(0, 7), (0, 2), (1, 2), (0, 3)],
    *[(1, 3), (1, 7), (0, 6), (3, 2)],
    *[(0, 5), (2, 7), (0, 4), (2, 6)],
    *[(1, 6), (3, 3), (2, 3), (3, 5)],
    *[(2, 2), (3, 7), (1, 5), (3, 6)],
    *[(1, 4), (2, 5), (3, 4), (2, 4)],
]


def pick(i, values):
    if len(values) == 1:
        return values[0]
    half = len(values) // 2
    return jnp.where(i < half, pick(i, values[:half]), pick(i - half, values[half:]))


def kernel(og_h, ig_h, va_h, go_h, lf_h, mf_h, *refs):
    tab_h = refs[:6]
    (go_o, gi_o, gv_o, gm_o, glr) = refs[6:11]
    (og, ig, va, go, lf, mf) = refs[11:17]
    tab = refs[17:23]
    (send, recv, send_f, recv_f, ret, back, gls) = refs[23:30]
    (in_sem, tab_sem, s1, r1, s2, r2, s3, r3, s4, r4, ready, here, near, far) = refs[30:]

    me = lax.axis_index("ctx")
    z = lax.axis_index("ch")
    chip = me // 2
    core = me % 2
    px, py = chip // 8, chip % 8

    def channel(x, y):
        return pick(x, [PLACES.index((i, y)) for i in range(4)])

    works = core == 1
    l = pick(py, [channel(px, y) for y in range(8)])
    leads = l < LEAD
    zo = l // 4
    hub = z == zo
    told = jnp.logical_and(zo < TOLD, z >= TOLD)
    bar = pltpu.get_barrier_semaphore()

    def signal(sem, ctx, ch):
        pl.semaphore_signal(sem, inc=1, device_id=(ctx, ch), device_id_type=MESH)

    def chip_at(dx, dy):
        return lax.rem(px + dx, 4) * 8 + lax.rem(py + dy, 8)

    @pl.when(core == 0)
    def _():
        signal(bar, me + 1, z)

    @pl.when(works)
    def _():
        for dx, dy in OFFSETS[:-1]:
            signal(bar, 2 * chip_at(dx, dy) + jnp.where(leads, 1, 0), z)

        @pl.when(jnp.logical_not(leads))
        def _():
            signal(bar, me - 1, z)

        @pl.when(z < zo)
        def _():
            signal(bar, me, zo)

        @pl.when(hub)
        def _():
            for p in range(1, 8):
                above = z < p if p < TOLD else jnp.logical_and(z < p, z >= TOLD)

                @pl.when(above)
                def _():
                    signal(bar, me, p)


    ins = [
        pltpu.make_async_copy(a, b, in_sem.at[i])
        for i, (a, b) in enumerate(
            [(ig_h, ig), (va_h, va), (go_h, go), (og_h, og), (lf_h, lf), (mf_h, mf)]
        )
    ]
    for c in ins:
        c.start()
    tabs = [pltpu.make_async_copy(a, b, tab_sem.at[i]) for i, (a, b) in enumerate(zip(tab_h, tab))]

    @pl.when(z < TOLD)
    def _():
        for p in range(TOLD, 8):
            for i in range(4):
                at = [PLACES[4 * q + i] for q in range(TOLD)]
                signal(bar, pick(z, [2 * (8 * x + y) + (1 if q < DIRECT else 0) for q, (x, y) in enumerate(at)]), p)

    @pl.when(works)
    def _():
        for c in tabs:
            c.start()

    for c in ins[:4]:
        c.wait()

    product = ig[...].astype(f32) * va[...].astype(f32)
    conv = go[...].astype(f32) * og[...].astype(f32)
    send[:, 0, :] = product[:, :W]
    send[:, 1, :] = product[:, W:]
    send[:, 2, :] = conv[:, :W]
    send[:, 3, :] = conv[:, W:]

    @pl.when(works)
    def _():
        from_below = jnp.where(hub, zo, jnp.where(z > zo, jnp.where(told, jnp.where(zo < DIRECT, 64, 0), 1), 0))
        pl.semaphore_wait(bar, LEAD + 1 - jnp.where(leads, 1, 0) + from_below)
        signal(near, me - 1, z)

        @pl.when(jnp.logical_and(z > zo, jnp.logical_not(told)))
        def _():
            signal(here, me, zo)

    def out(src, dst, ssem, rsem, d, p):
        pltpu.make_async_remote_copy(
            src_ref=src,
            dst_ref=dst,
            send_sem=ssem,
            recv_sem=rsem,
            device_id=(d, p),
            device_id_type=MESH,
        ).start()

    def put_all(src, dst, ssem, rsem, channels):
        def put(x, y):
            out(src.at[channel(x, y)], dst.at[me], ssem, rsem, 2 * (8 * x + y) + 1, z)

        def put_near(x, y):
            mine = jnp.logical_and(works, jnp.logical_and(px == x, py == y))
            pl.when(jnp.logical_not(mine))(functools.partial(put, x, y))

        chips = [PLACES[i] for i in channels]
        rows = [y for y in range(8) if all((x, y) in chips for x in range(4))]
        for dx in (2, 1, 3):
            for y in rows:
                put(lax.rem(px + dx, 4), y)
        for y in rows:
            put_near(px, y)
        for x, y in chips:
            if y not in rows:
                put_near(x, y)

    @pl.when(core == 0)
    def _():
        pl.semaphore_wait(near, 1)

    put_all(send, recv, s1, r1, range(LEAD))

    @pl.when(core == 0)
    def _():
        pl.semaphore_wait(bar, 32 - LEAD + jnp.where(jnp.logical_and(told, zo >= DIRECT), 64, 0))
        signal(far, me + 1, z)

    @pl.when(works)
    def _():
        pl.semaphore_wait(far, 1)

    put_all(send, recv, s1, r1, range(LEAD, 32))
    for c in ins[4:]:
        c.wait()
    filt = lf[...]
    send_f[:, 0, :] = filt[:, :W]
    send_f[:, 1, :] = filt[:, W:]
    put_all(send_f, recv_f, s4, r4, range(32))

    @pl.when(works)
    def _():
        pltpu.make_async_copy(send.at[l], recv.at[me], r1).start()
        pltpu.make_async_copy(send_f.at[l], recv_f.at[me], r4).start()

        for c in tabs:
            c.wait()
        (w1, w2, w3, w4, tcr, tsr) = tab
        tc, ts = tcr[...], tsr[...]
        row = lax.broadcasted_iota(jnp.int32, (W, W), 0)
        col = lax.broadcasted_iota(jnp.int32, (W, W), 1)
        upper = col >= row
        half_row = lax.broadcasted_iota(jnp.int32, (64, W), 0)
        k = jnp.broadcast_to(mf[pl.ds(l, 1), :], (W, W))
        rolled = pltpu.roll(k, 0, 1, stride=1, stride_axis=0)
        k0 = split(jnp.where(upper, rolled, 0.0))
        k1 = split(jnp.where(upper, 0.0, rolled))

        pltpu.make_async_copy(recv, recv, r1).wait()

        @pl.when(hub)
        def _():
            for p in range(7):
                @pl.when(p < z)
                def _():
                    signal(ready, me, p)

        def ready_above():
            top = jnp.where(zo < TOLD, TOLD - 1, 7)

            @pl.when(z < top)
            def _():
                pl.semaphore_wait(here, top - z)

            for p in range(7, 0, -1):
                @pl.when(jnp.logical_and(z < p, p <= top))
                def _():
                    signal(ready, me, p)

        pl.when(jnp.logical_and(hub, zo >= TOLD))(ready_above)

        def forward(x):
            s = dot(w1[...], data([split(x)], 0))
            re, im = s[:W], s[W:]
            t = jnp.concatenate([re * tc + im * ts, im * tc - re * ts], 1)
            t = dot(data([split(t)], 1), w2[...])
            return t[:, :W], t[:, W:]

        def inverse(y):
            t = dot(data([split(y)], 1), w3[...])
            parts = []
            for i in range(y.shape[0] // W):
                re, im = t[i * W : (i + 1) * W, :W], t[i * W : (i + 1) * W, W:]
                parts.append(jnp.concatenate([re * tc - im * ts, im * tc + re * ts], 0))
            return dot(w4[...], data([split(jnp.concatenate(parts, 1))], 0))

        def times(a, b):
            return jnp.concatenate([a[0] * b[0] - a[1] * b[1], a[0] * b[1] + a[1] * b[0]], 1)

        def times_conj(a, b):
            return jnp.concatenate([a[0] * b[0] + a[1] * b[1], a[1] * b[0] - a[0] * b[1]], 1)

        c = forward(jnp.concatenate([recv[:, 2, :], recv[:, 3, :]], 0))
        pe, po = recv[:, 0, :], recv[:, 1, :]
        po_prev = jnp.where(half_row == 0, 0.0, pltpu.roll(po, 1, 0))
        p0 = split(jnp.concatenate([pe, po], 0))
        p1 = split(jnp.concatenate([po_prev, pe], 0))
        m = forward(dot(data([p0, p1], 1), taps([k0, k1], 0)))
        slot = z * 4 + l % 4

        def long_gradient():
            glong = inverse(times_conj(c, m)) * (N**-0.5)
            gls[:, 0, :] = glong[:64]
            gls[:, 1, :] = glong[64:]

            @pl.when(jnp.logical_not(jnp.logical_or(hub, told)))
            def _():
                pl.semaphore_wait(ready, 1)

            def put(d):
                out(gls.at[d], glr.at[slot], s3, r3, d, zo)

            for i in CHIPS:
                put(2 * i + 1 - core)
                pl.when(jnp.logical_not(jnp.logical_and(hub, chip == i)))(
                    functools.partial(put, 2 * i + core)
                )

            @pl.when(hub)
            def _():
                pltpu.make_async_copy(gls.at[me], glr.at[slot], r3).start()

        soon = jnp.logical_and(z >= zo, z >= 3)
        pl.when(soon)(long_gradient)

        pltpu.make_async_copy(recv_f, recv_f, r4).wait()
        h = forward(jnp.concatenate([recv_f[:, 0, :], recv_f[:, 1, :]], 0))
        both = inverse(jnp.concatenate([times(m, h), times_conj(c, h)], 0))
        recon, gmix = both[:, :W], both[:, W:]
        ge, gd = gmix[:64], gmix[64:]
        ge_next = jnp.where(half_row == 63, 0.0, pltpu.roll(ge, 63, 0))
        g0 = split(gmix)
        g1 = split(jnp.concatenate([gd, ge_next], 0))
        gprod = dot(data([g0, g1], 1), taps([k0, k1], 1), NT)
        g3 = taps([g0], 0)
        d = jnp.where(upper, dot(data([p0], 0), g3, TN), dot(data([p1], 0), g3, TN))
        for bit in range(7):
            moved = pltpu.roll(d, W - (1 << bit), 1)
            d = jnp.where((row >> bit) & 1 == 1, moved, d)
        gmid = jnp.sum(d, 0, keepdims=True) * (N**-0.5)

        ret[:, 0, :] = recon[:64]
        ret[:, 1, :] = recon[64:]
        ret[:, 2, :] = gprod[:64]
        ret[:, 3, :] = gprod[64:]
        ret[:, 4, :] = jnp.broadcast_to(gmid, (64, W))

        def put_back(d):
            out(ret.at[d], back.at[l], s2, r2, d, z)

        for i in CHIPS:
            put_back(2 * i + 1 - core)
            pl.when(chip != i)(functools.partial(put_back, 2 * i + core))
        pltpu.make_async_copy(ret.at[me], back.at[l], r2).start()

        pl.when(jnp.logical_and(hub, zo < TOLD))(ready_above)
        pl.when(jnp.logical_not(soon))(long_gradient)

    def left(ref, count, sem):
        part = ref.at[pl.ds(0, count)]
        pltpu.make_async_copy(part, part, sem).wait()

    left(send, 31, s1)
    left(send_f, 31, s4)

    @pl.when(jnp.logical_not(works))
    def _():
        left(send, 1, s1)
        left(send_f, 1, s4)

    @pl.when(works)
    def _():
        left(gls, 63, s3)
        left(ret, 63, s2)

        @pl.when(jnp.logical_not(hub))
        def _():
            left(gls, 1, s3)

    pltpu.make_async_copy(back, back, r2).wait()
    recon = jnp.concatenate([back[:, 0, :], back[:, 1, :]], 1)
    gprod = jnp.concatenate([back[:, 2, :], back[:, 3, :]], 1)
    go_o[...] = (go[...].astype(f32) * recon).astype(bf16)
    gi_o[...] = (gprod * va[...].astype(f32)).astype(bf16)
    gv_o[...] = (gprod * ig[...].astype(f32)).astype(bf16)
    gm_o[...] = back[:, 4, :]
    pltpu.make_async_copy(glr, glr, r3).wait()


def deliver(a, b, c, m, parts, a_o, b_o, c_o, gl_o, m_o, gl, sem):
    copies = [
        pltpu.make_async_copy(x, y, sem.at[i])
        for i, (x, y) in enumerate([(a, a_o), (b, b_o), (c, c_o), (m, m_o), (gl, gl_o)])
    ]
    for copy in copies[:4]:
        copy.start()
    total = parts[0:4]
    for i in range(1, 8):
        total = total + parts[4 * i : 4 * i + 4]
    gl[:, :W] = total[:, 0, :]
    gl[:, W:] = total[:, 1, :]
    copies[4].start()
    for copy in copies:
        copy.wait()


def local(outer_gate, inner_gate, values, grad_out, long_filter, mid_filter):
    tabs = tables()
    vm = pltpu.VMEM
    dma = pltpu.SemaphoreType.DMA
    hbm = pl.BlockSpec(memory_space=pl.ANY)
    vmem = pl.BlockSpec(memory_space=vm)
    ins = (outer_gate, inner_gate, values, grad_out, long_filter, mid_filter)
    outs = [((32, 256), bf16)] * 3 + [((32, W), f32)]
    shapes = [jax.ShapeDtypeStruct(*o) for o in outs]
    ins = [pltpu.with_memory_space_constraint(a, pltpu.HBM) for a in (*ins, *map(jnp.asarray, tabs))]
    results = pl.pallas_call(
        kernel,
        out_shape=[*[vm(*o) for o in outs], vm((32, 2, W), f32)],
        in_specs=[hbm] * 12,
        out_specs=[vmem] * 5,
        scratch_shapes=[
            *[vm((32, 256), bf16)] * 4,
            vm((32, 256), f32),
            vm((32, W), f32),
            *[vm(t.shape, t.dtype) for t in tabs],
            vm((32, 4, W), f32),
            vm((64, 4, W), f32),
            vm((32, 2, W), f32),
            vm((64, 2, W), f32),
            vm((64, 5, W), f32),
            vm((32, 5, W), f32),
            vm((64, 2, W), f32),
            dma((6,)),
            dma((6,)),
            *[dma] * 8,
            *[pltpu.SemaphoreType.REGULAR] * 4,
        ],
        compiler_params=pltpu.CompilerParams(
            collective_id=0, has_side_effects=True, vmem_limit_bytes=VMEM_BYTES
        ),
    )(*ins)
    return pl.pallas_call(
        deliver,
        out_shape=[*shapes[:3], jax.ShapeDtypeStruct((4, 256), f32), shapes[3]],
        in_specs=[vmem] * 5,
        out_specs=[hbm] * 5,
        scratch_shapes=[vm((4, 256), f32), dma((5,))],
        compiler_params=pltpu.CompilerParams(vmem_limit_bytes=VMEM_BYTES),
    )(*results)


def solution(mesh):
    in_specs = (
        P("ch", "ctx"),
        P("ch", "ctx"),
        P("ch", "ctx"),
        P("ch", "ctx"),
        P(None, "ctx"),
        P("ch", None),
    )
    out_specs = (P("ch", "ctx"), P("ch", "ctx"), P("ch", "ctx"), P("ch", "ctx"), P("ch", None))
    return jax.shard_map(local, mesh=mesh, in_specs=in_specs, out_specs=out_specs, check_vma=False)
```
